512 devices in a mesh: delay: 16 (over y, core), row: 32 (over z, x).
Axes of the slice: x: 4, y: 8, z: 8, core: 2. Of those that a mesh axis runs over, the one named last changes fastest.
Arguments:
- incident: bfloat16 [64, 4096], P(None, 'row'), may hold values from -12 to 12
- onset: int32 [64], replicated, may hold values from 0 to 2
- beta: float32 [4096], P('delay'), may hold values from 0.05 to 0.5
- inverse_block: bfloat16 [4096, 4096], P('row', 'delay'), may hold values from -0.0625 to 0.0625
- delay_blocks: bfloat16 [16, 4096, 4096], P('delay', None, 'row'), may hold values from -0.09375 to 0.09375
- history_sum: float32 [16, 64, 4096], P('delay', None, 'row'), may hold values from -12 to 12
Outputs:
- currents: bfloat16 [3, 64, 4096], P(None, None, 'delay')
- carried: float32 [16, 64, 4096], P('delay', None, 'row')
The draws below stay inside these ranges and needn't reach their ends.
All inputs are finite; a program needn't handle non-finite values.
Results may differ from the reference program's by a relative error of at most 0.0056.
Values may be sent and summed in bfloat16 or wider, within the bound.
A program may use at most 64 MiB of HBM per device.

```python
import math
import jax
import jax.numpy as jnp
from jax import lax

N = 4096
E = 64
STEPS = 3
DELAYS = 16


def set_ends(result, stream_key, least, largest):
    longest = result.shape.index(max(result.shape))
    spots = []
    for shift in (0, 1):
        where = [jax.random.randint(jax.random.fold_in(stream_key, axis), (), 0, length) for axis, length in enumerate(result.shape)]
        where[longest] = (where[longest] + shift) % result.shape[longest]
        spots.append(tuple(where))
    return result.at[spots[0]].set(least).at[spots[1]].set(largest)


def block_levels(stream_key, dims, cuts, least, top_value):
    loudness = 1.0
    for axis_at, shards_of in cuts:
        draws = jax.random.uniform(jax.random.fold_in(jax.random.fold_in(stream_key, 6), axis_at), (shards_of,), jnp.float32, least / len(cuts), top_value / len(cuts))
        loudness = loudness * jnp.repeat(jnp.exp(draws), dims[axis_at] // shards_of).reshape((-1,) + (1,) * (len(dims) - 1 - axis_at))
    return loudness


def noise(key, shape, deviation, most, shards=(), dtype=jnp.bfloat16):
    level = block_levels(key, shape, shards, -0.22, 0.18) if shards else 1.0
    entries = jax.random.normal(key, shape, jnp.float32) * deviation * level
    return jnp.minimum(jnp.maximum(entries, -most), most).astype(dtype)


def setup_inputs(seed: int = 0) -> dict:
    streams_of = jax.random.split(jax.random.key(seed), 7)
    incident = noise(streams_of[0], (E, N), 2.0, 12.0, ((1, 32),))
    onset = set_ends(jax.random.randint(streams_of[1], (E,), 0, STEPS), jax.random.fold_in(streams_of[1], 1), 0, STEPS - 1).astype(jnp.int32)
    beta = jnp.clip(jnp.exp(math.log(0.5) - 2.3025851 * jax.random.uniform(streams_of[2], (N,), jnp.float32) ** block_levels(streams_of[2], (N,), ((0, 16),), -0.2, 0.2)), 0.05, 0.5)
    inverse_block = noise(streams_of[3], (N, N), (2 * N) ** -0.5, 0.0625, ((0, 32), (1, 16)))
    delay_blocks = noise(streams_of[4], (DELAYS, N, N), N ** -0.5, 0.09375, ((0, 16), (2, 32)))
    history_sum = noise(streams_of[5], (DELAYS, E, N), 2.0, 12.0, ((0, 16), (2, 32)), jnp.float32)
    return dict(incident=incident, onset=onset, beta=beta, inverse_block=inverse_block, delay_blocks=delay_blocks, history_sum=history_sum)


def reference(incident, onset, beta, inverse_block, delay_blocks, history_sum):
    delay_wide = delay_blocks.astype(jnp.float32)
    incident_wide = incident.astype(jnp.float32)
    future = history_sum
    outputs = []
    for step_index in range(STEPS):
        offset_time = (step_index - onset).astype(jnp.float32)
        envelope = jnp.where(offset_time >= 0.0, jnp.exp(-(offset_time - 1.0) ** 2 / 4.0), 0.0)
        drive = incident_wide * envelope[:, None]
        residual = (drive - future[0]).astype(jnp.bfloat16)
        solved = jnp.dot(residual, inverse_block, preferred_element_type=jnp.float32)
        current = (solved / (1.0 + beta[None, :] * solved * solved)).astype(jnp.bfloat16)
        outputs.append(current)
        contrib = jnp.einsum("en,knm->kem", current.astype(jnp.float32), delay_wide, precision=lax.Precision.HIGHEST)
        future = jnp.concatenate([future[1:], jnp.zeros_like(future[:1])], axis=0) + contrib
    return jnp.stack(outputs), future
```

```python
import jax
import jax.numpy as jnp
from jax import lax
from jax.experimental import pallas as pl
from jax.experimental.pallas import tpu as pltpu
from jax.sharding import PartitionSpec as P

STEPS = 3
MESH = pl.DeviceIdType.MESH
F32, BF16 = jnp.float32, jnp.bfloat16
NY, NC, NZ, NX = 8, 2, 8, 4
NQ = NX * NC
ROWS = 8


def kernel(
    incident, onset, beta, inverse, matrix, history,
    currents, carried,
    inc_v, mat_v, inv_v, dl_v, stage_v, beta_v, hb_v, base_v, zbuf, xbuf, c_all, passed, future, cur_v,
    load_sem, send_sem, recv_sem, z_send, z_recv, x_send, x_recv, c_send, c_recv, p_send, p_recv, out_sem,
):
    d, r = lax.axis_index("delay"), lax.axis_index("row")
    y, c = d // NC, d % NC
    z, x = r // NX, r % NX
    q = x * NC + c
    slab = y * NQ + q

    def at(ty, tc, tz, tx):
        return (ty * NC + tc, tz * NX + tx)

    def at_slab(i):
        t = lax.rem(slab + i, NY * NQ)
        ty, tq = t // NQ, t % NQ
        return at(ty, tq % NC, z, tq // NC)

    def at_z(i):
        return at(y, c, lax.rem(z + i, NZ), x)

    def at_q(i):
        tq = lax.rem(q + i, NQ)
        return at(y, tq % NC, z, tq // NC)

    def at_x(i):
        return at(y, c, z, lax.rem(x + i, NX))

    def remote(src, dst, send, recv, target):
        return pltpu.make_async_remote_copy(
            src_ref=src, dst_ref=dst, send_sem=send, recv_sem=recv, device_id=target, device_id_type=MESH
        )

    def arrived(ref, sem):
        pltpu.make_async_copy(ref, ref, sem).wait()

    load_inc = pltpu.make_async_copy(incident, inc_v, load_sem.at[0])
    load_inc.start()
    load_mat = pltpu.make_async_copy(matrix.at[0], mat_v, load_sem.at[1])
    load_mat.start()

    barrier = pltpu.get_barrier_semaphore()

    def greet_slab(i, _):
        pl.semaphore_signal(barrier, inc=1, device_id=at_slab(i), device_id_type=MESH)
        return 0

    def greet_z(i, _):
        pl.semaphore_signal(barrier, inc=1, device_id=at_z(i), device_id_type=MESH)
        return 0

    lax.fori_loop(1, NZ, greet_z, 0)
    lax.fori_loop(1, NY * NQ, greet_slab, 0)
    pl.semaphore_wait(barrier, NZ - 1 + NY * NQ - 1)

    for s in range(STEPS):

        @pl.when(d == s)
        def _(s=s):
            def send(i, _):
                t = lax.rem(d + i, NY * NC)
                rows = pl.ds(pl.multiple_of(t // NC * ROWS, ROWS), ROWS)
                remote(history.at[0, rows], hb_v.at[s], send_sem.at[0], recv_sem.at[s], (t, r)).start()
                return 0

            lax.fori_loop(1, NY * NC, send, 0)
            own = pl.ds(pl.multiple_of(y * ROWS, ROWS), ROWS)
            pltpu.make_async_copy(history.at[0, own], hb_v.at[s], recv_sem.at[s]).start()

    qy_c, qy_x = y % NC, y // NC

    def spread(src, dst, send, recv):
        def one(i, _):
            t = lax.rem(y + i, NY)
            here = jnp.logical_and(t == y, q == y)

            @pl.when(here)
            def _():
                pltpu.make_async_copy(src, dst, recv).start()

            @pl.when(jnp.logical_not(here))
            def _():
                remote(src, dst, send, recv, at(t, qy_c, z, qy_x)).start()

            return 0

        lax.fori_loop(0, NY, one, 0)

    def spread_done(src, send):
        def one(i, _):
            @pl.when(jnp.logical_not(jnp.logical_and(i == 0, q == y)))
            def _():
                pltpu.make_async_copy(src, src, send).wait()

            return 0

        lax.fori_loop(0, NY, one, 0)

    x_rows = pl.ds(pl.multiple_of(x * 128, 128), 128)
    c_cols = pl.ds(pl.multiple_of(c * 256, 256), 256)
    spread(inverse, inv_v.at[x_rows, c_cols], send_sem.at[1], recv_sem.at[3])

    @pl.when(x == 0)
    def _():
        spread(beta, beta_v.at[c], send_sem.at[2], recv_sem.at[4])

    for k in range(2):

        @pl.when(d == k)
        def _(k=k):
            def send(i, _):
                t = lax.rem(d + i, NY * NC)
                rows = pl.ds(pl.multiple_of(t * 256, 256), 256)
                remote(matrix.at[0, rows], stage_v.at[k], send_sem.at[3], recv_sem.at[5 + k], (t, r)).start()
                return 0

            lax.fori_loop(1, NY * NC, send, 0)
            own = pl.ds(pl.multiple_of(d * 256, 256), 256)
            pltpu.make_async_copy(matrix.at[0, own], stage_v.at[k], recv_sem.at[5 + k]).start()

    def pass_on(src, k):
        @pl.when(d > 0)
        def _():
            remote(src, passed.at[k], p_send.at[k], p_recv.at[k], (jnp.maximum(d - 1, 0), r)).start()

    def take(k):
        @pl.when(d < NY * NC - 1)
        def _():
            arrived(passed.at[k], p_recv.at[k])

        return jnp.where(d < NY * NC - 1, passed[k], 0.0)

    pass_on(history.at[0], 0)

    load_inc.wait()
    future[0] = inc_v[...].astype(F32)
    own_rows = pl.ds(pl.multiple_of(y * ROWS, ROWS), ROWS)
    wide = future[0, own_rows]
    row_of = lax.broadcasted_iota(jnp.int32, (ROWS, 128), 0)
    start = jnp.zeros((ROWS, 128), jnp.int32)
    for e in range(ROWS):
        start = jnp.where(row_of == e, onset[y * ROWS + e], start)
    for s in range(STEPS):
        offset = (s - start).astype(F32)
        envelope = jnp.where(offset >= 0.0, jnp.exp(-((offset - 1.0) ** 2) / 4.0), 0.0)
        arrived(hb_v.at[s], recv_sem.at[s])
        base_v[x, s] = wide * envelope - hb_v[s]
    for i in range(1, NX):
        remote(base_v.at[x], base_v.at[x], send_sem.at[4], recv_sem.at[7], at_x(i)).start()
    arrived(base_v.at[pl.ds(0, NX - 1)], recv_sem.at[7])

    def base(s):
        return jnp.concatenate([base_v[i, s] for i in range(NX)], axis=1)

    def forward(k):
        arrived(stage_v.at[k], recv_sem.at[5 + k])
        rows = pl.ds(pl.multiple_of(c * 256, 256), 256)
        cols = pl.ds(pl.multiple_of(x * 128, 128), 128)
        spread(stage_v.at[k], dl_v.at[k, rows, cols], send_sem.at[5 + k], recv_sem.at[8 + k])

    def product(s):
        arrived(c_all.at[s, pl.ds(0, (NY * NQ - 1) * 16)], c_recv.at[s])
        total = jnp.zeros((64, 128), F32)
        for qq in range(NQ):
            block = c_all[s, pl.ds(qq * 128, 128)].astype(F32).reshape(NY, 2, ROWS, 256)
            for half in range(2):
                values = block[:, half].reshape(64, 256).astype(BF16)
                total += jnp.dot(values, mat_v[pl.ds(qq * 512 + half * 256, 256)], preferred_element_type=F32)
        block = c_all[s, pl.ds(pl.multiple_of(y * 128, 128), 128)].astype(F32).reshape(NY, 2, ROWS, 256)
        cur_v[s] = jnp.where(c == 0, block[:, 0], block[:, 1]).reshape(64, 256).astype(BF16)
        pltpu.make_async_copy(cur_v.at[s], currents.at[s], out_sem.at[s]).start()
        return total

    forward(0)
    earlier = jnp.zeros((ROWS, 512), F32)
    residual = base(0)
    for s in range(STEPS):
        if s == 0:
            arrived(inv_v, recv_sem.at[3])
        zbuf[s, z] = jnp.dot(residual.astype(BF16), inv_v[...], preferred_element_type=F32)
        for i in range(1, NZ):
            remote(zbuf.at[s, z], zbuf.at[s, z], z_send.at[s], z_recv.at[s], at_z(i)).start()
        if s == 0:
            forward(1)
            arrived(beta_v, recv_sem.at[4])
        if s == 1:
            arrived(dl_v.at[1], recv_sem.at[9])
            earlier = jnp.dot(current.astype(BF16), dl_v[1], preferred_element_type=F32)
        if s == 2:
            load_mat.wait()
            future[0] = take(0) + product(0)
            pass_on(future.at[0], 1)
        arrived(zbuf.at[s, pl.ds(0, NZ - 1)], z_recv.at[s])
        solved = zbuf[s, 0]
        for i in range(1, NZ):
            solved += zbuf[s, i]
        beta_wide = jnp.concatenate([beta_v[0], beta_v[1]], axis=1)
        current = (solved / (1.0 + beta_wide * solved * solved)).astype(BF16).astype(F32)
        mine = pl.ds(pl.multiple_of(q * 128 + y * 16, 16), 16)
        c_all[s, mine] = jnp.concatenate([current[:, :256], current[:, 256:]], axis=0).astype(BF16)
        if s < STEPS - 1:
            if s == 0:
                arrived(dl_v.at[0], recv_sem.at[8])
            xbuf[s, q] = jnp.dot(current.astype(BF16), dl_v[0], preferred_element_type=F32) + earlier
            for i in range(1, NQ):
                remote(xbuf.at[s, q], xbuf.at[s, q], x_send.at[s], x_recv.at[s], at_q(i)).start()

        def send_values(i, _):
            remote(c_all.at[s, mine], c_all.at[s, mine], c_send.at[s], c_recv.at[s], at_slab(i)).start()
            return 0

        lax.fori_loop(1, NY * NQ, send_values, 0)
        if s < STEPS - 1:
            arrived(xbuf.at[s, pl.ds(0, NQ - 1)], x_recv.at[s])
            total = xbuf[s, 0]
            for i in range(1, NQ):
                total += xbuf[s, i]
            residual = base(s + 1) - total

    future[1] = take(1) + product(1)
    pass_on(future.at[1], 2)
    future[2] = product(2)
    future[2] = future[2] + take(2)
    out = pltpu.make_async_copy(future.at[2], carried.at[0], out_sem.at[STEPS])
    out.start()

    for s in range(STEPS):
        @pl.when(d == s)
        def _():
            def one(i, _):
                pltpu.make_async_copy(hb_v.at[0], hb_v.at[0], send_sem.at[0]).wait()
                return 0

            lax.fori_loop(1, NY * NC, one, 0)

        pltpu.make_async_copy(zbuf.at[s, pl.ds(0, NZ - 1)], zbuf.at[s, pl.ds(0, NZ - 1)], z_send.at[s]).wait()
        sent = c_all.at[s, pl.ds(0, (NY * NQ - 1) * 16)]
        pltpu.make_async_copy(sent, sent, c_send.at[s]).wait()
        if s < STEPS - 1:
            sent = xbuf.at[s, pl.ds(0, NQ - 1)]
            pltpu.make_async_copy(sent, sent, x_send.at[s]).wait()

        @pl.when(d > 0)
        def _(s=s):
            pltpu.make_async_copy(passed.at[s], passed.at[s], p_send.at[s]).wait()

        pltpu.make_async_copy(cur_v.at[s], currents.at[s], out_sem.at[s]).wait()
    spread_done(inverse, send_sem.at[1])

    @pl.when(x == 0)
    def _():
        spread_done(beta, send_sem.at[2])

    for k in range(2):
        @pl.when(d == k)
        def _():
            def one(i, _):
                pltpu.make_async_copy(stage_v.at[0], stage_v.at[0], send_sem.at[3]).wait()
                return 0

            lax.fori_loop(1, NY * NC, one, 0)

        spread_done(stage_v.at[k], send_sem.at[5 + k])
    sent = base_v.at[pl.ds(0, NX - 1)]
    pltpu.make_async_copy(sent, sent, send_sem.at[4]).wait()
    out.wait()


def per_device(incident, onset, beta, inverse_block, delay_blocks, history_sum):
    anywhere = pl.BlockSpec(memory_space=pl.ANY)
    dma = pltpu.SemaphoreType.DMA
    return pl.pallas_call(
        kernel,
        out_shape=(
            jax.ShapeDtypeStruct((STEPS, 64, 256), BF16),
            jax.ShapeDtypeStruct((1, 64, 128), F32),
        ),
        in_specs=[anywhere, pl.BlockSpec(memory_space=pltpu.SMEM), anywhere, anywhere, anywhere, anywhere],
        out_specs=(anywhere, anywhere),
        scratch_shapes=[
            pltpu.VMEM((64, 128), BF16),
            pltpu.VMEM((4096, 128), BF16),
            pltpu.VMEM((512, 512), BF16),
            pltpu.VMEM((2, 512, 512), BF16),
            pltpu.VMEM((2, 256, 128), BF16),
            pltpu.VMEM((NC, 1, 256), F32),
            pltpu.VMEM((STEPS, ROWS, 128), F32),
            pltpu.VMEM((NX, STEPS, ROWS, 128), F32),
            pltpu.VMEM((STEPS, NZ, ROWS, 512), F32),
            pltpu.VMEM((STEPS, NQ, ROWS, 512), F32),
            pltpu.VMEM((STEPS, NY * NQ * 16, 256), BF16),
            pltpu.VMEM((STEPS, 64, 128), F32),
            pltpu.VMEM((STEPS, 64, 128), F32),
            pltpu.VMEM((STEPS, 64, 256), BF16),
            dma((4,)),
            dma((7,)),
            dma((10,)),
            dma((STEPS,)),
            dma((STEPS,)),
            dma((STEPS,)),
            dma((STEPS,)),
            dma((STEPS,)),
            dma((STEPS,)),
            dma((STEPS,)),
            dma((STEPS,)),
            dma((STEPS + 1,)),
        ],
        compiler_params=pltpu.CompilerParams(
            collective_id=0, has_side_effects=True, vmem_limit_bytes=24 * 2**20
        ),
    )(incident, onset, beta.reshape(1, 256), inverse_block, delay_blocks, history_sum)


def solution(mesh):
    placed = (
        P(None, "row"),
        P(),
        P("delay"),
        P("row", "delay"),
        P("delay", None, "row"),
        P("delay", None, "row"),
    )
    return jax.shard_map(
        per_device,
        mesh=mesh,
        in_specs=placed,
        out_specs=(P(None, None, "delay"), P("delay", None, "row")),
        check_vma=False,
    )
```

```python
import jax
import jax.numpy as jnp
from jax import lax
from jax.experimental import pallas as pl
from jax.experimental.pallas import tpu as pltpu
from jax.sharding import PartitionSpec as P

STEPS = 3
MESH = pl.DeviceIdType.MESH
F32, BF16 = jnp.float32, jnp.bfloat16
NY, NC, NZ, NX = 8, 2, 8, 4
ND = NY * NC
ROWS = 16


def far_first(n):
    return sorted(range(n), key=lambda i: -min(i, n - i))


LINE = [i for i in far_first(NZ) if i]
SLAB = [(dy, dc, dx) for dy in far_first(NY) for dx in far_first(NX) for dc in range(NC) if (dy, dc, dx) != (0, 0, 0)]
SLAB.sort(key=lambda o: -min(o[0], NY - o[0]) - min(o[2], NX - o[2]))
CORE = [o for o in SLAB if o[1] == 0]
DELAY = [o for o in SLAB if o[2] == 0]
OTHER_X = [i for i in far_first(NX) if i]


def kernel(
    incident, onset, beta, inverse, matrix, history,
    currents, carried,
    inc_v, hist_v, mat_v, inv_v, dl_v, stage_v, beta_v, first_v, res_v, base_v, zbuf, pre_v, xbuf, c_own, c_all,
    passed, future, first_src,
    load_sem, send_sem, recv_sem, z_send, z_recv, h_send, h_recv, x_send, x_recv, c_send, c_recv, m_send, m_recv,
    p_send, p_recv,
):
    d, r = lax.axis_index("delay"), lax.axis_index("row")
    y, c = d // NC, d % NC
    z, x = r // NX, r % NX

    def at(dy=0, dc=0, dz=0, dx=0):
        ty = lax.rem(y + dy, NY) if dy else y
        tc = 1 - c if dc else c
        tz = lax.rem(z + dz, NZ) if dz else z
        tx = lax.rem(x + dx, NX) if dx else x
        return (ty * NC + tc, tz * NX + tx)

    def remote(src, dst, send, recv, target):
        return pltpu.make_async_remote_copy(
            src_ref=src, dst_ref=dst, send_sem=send, recv_sem=recv, device_id=target, device_id_type=MESH
        )

    def arrived(ref, sem):
        pltpu.make_async_copy(ref, ref, sem).wait()

    left = arrived

    def rows_of(tx):
        return pl.ds(pl.multiple_of(tx * ROWS, ROWS), ROWS)

    own_rows = rows_of(x)

    loads = [
        pltpu.make_async_copy(src, dst, load_sem.at[i])
        for i, (src, dst) in enumerate(
            ((incident, inc_v), (history.at[0], hist_v), (beta, beta_v), (matrix.at[0], mat_v))
        )
    ]
    for load in loads:
        load.start()

    barrier = pltpu.get_barrier_semaphore()
    for i in LINE:
        pl.semaphore_signal(barrier, inc=1, device_id=at(dz=i), device_id_type=MESH)
    for dy, dc, dx in SLAB:
        pl.semaphore_signal(barrier, inc=1, device_id=at(dy, dc, 0, dx), device_id_type=MESH)

    for load in loads[:3]:
        load.wait()

    @pl.when(d < STEPS)
    def _():
        row_of = lax.broadcasted_iota(jnp.int32, (8, 128), 0)
        start = []
        for i in range(0, 64, 8):
            group = jnp.zeros((8, 128), jnp.int32)
            for e in range(8):
                group = jnp.where(row_of == e, onset[i + e], group)
            start.append(group)
        offset = (d - jnp.concatenate(start, axis=0)).astype(F32)
        envelope = jnp.where(offset >= 0.0, jnp.exp(-((offset - 1.0) ** 2) / 4.0), 0.0)
        res_v[...] = inc_v[...].astype(F32) * envelope - hist_v[...]
        first_src[...] = res_v[...].astype(BF16)

    pl.semaphore_wait(barrier, len(LINE) + len(SLAB))


    def cut(k):
        for dy, dc, dx in DELAY:
            t, tr = at(dy, dc)
            rows = pl.ds(pl.multiple_of(t * 256, 256), 256)
            remote(matrix.at[0, rows], stage_v.at[k], send_sem.at[1], recv_sem.at[1 + k], (t, tr)).start()
        pltpu.make_async_copy(matrix.at[0, pl.ds(k * 256, 256)], stage_v.at[k], recv_sem.at[1 + k]).start()

    def forward(k):
        arrived(stage_v.at[k], recv_sem.at[1 + k])
        columns = pl.ds(pl.multiple_of(x * 128, 128), 128)
        for i in OTHER_X:
            remote(stage_v.at[k], dl_v.at[k, :, columns], send_sem.at[4], recv_sem.at[3 + k], at(dx=i)).start()
        pltpu.make_async_copy(stage_v.at[k], dl_v.at[k, :, columns], recv_sem.at[3 + k]).start()

    @pl.when(d == 0)
    def _():
        for dy, dc, dx in SLAB:
            t = at(dy, dc, 0, dx)
            rows = rows_of(lax.rem(x + dx, NX)) if dx else own_rows
            remote(first_src.at[rows], first_v.at[x], send_sem.at[0], recv_sem.at[0], t).start()
        pltpu.make_async_copy(first_src.at[own_rows], first_v.at[x], recv_sem.at[0]).start()
        cut(0)

    inv_rows = pl.ds(pl.multiple_of(x * 128, 128), 128)
    for i in OTHER_X:
        remote(inverse, inv_v.at[inv_rows], send_sem.at[2], recv_sem.at[5], at(dx=i)).start()
    pltpu.make_async_copy(inverse, inv_v.at[inv_rows], recv_sem.at[5]).start()

    @pl.when(jnp.logical_and(d > 0, d < STEPS))
    def _():
        base_v[x] = res_v[own_rows]
        for i in OTHER_X:
            rows = rows_of(lax.rem(x + i, NX))
            remote(res_v.at[rows], base_v.at[x], send_sem.at[3], recv_sem.at[6], at(dx=i)).start()

    def pass_on(src, k):
        @pl.when(d > 0)
        def _():
            remote(src, passed.at[k], p_send.at[k], p_recv.at[k], (jnp.maximum(d - 1, 0), r)).start()

    def take(k):
        @pl.when(d < ND - 1)
        def _():
            arrived(passed.at[k], p_recv.at[k])

        return jnp.where(d < ND - 1, passed[k], 0.0)

    def share(s):
        arrived(c_all.at[s, c], c_recv.at[s])
        remote(c_all.at[s, c], c_all.at[s, c], m_send.at[s], m_recv.at[s], at(dc=1)).start()
        currents[s] = c_all[s, c, :, own_columns]

    own_columns = pl.ds(pl.multiple_of(y * 256, 256), 256)

    def product(s):
        total = jnp.zeros((64, 128), F32)
        for core in (c, 1 - c):
            if core is not c:
                arrived(c_all.at[s, core], m_recv.at[s])
            values = c_all[s, core]
            for i in range(NY):
                rows = pl.ds(pl.multiple_of((NC * i + core) * 256, 256), 256)
                total += jnp.dot(values[:, i * 256 : (i + 1) * 256], mat_v[rows], preferred_element_type=F32)
        return total

    def side_by_side(blocks):
        return jnp.concatenate([blocks[i].astype(F32) for i in range(NX)], axis=1)

    arrived(first_v, recv_sem.at[0])
    residual = side_by_side(first_v)
    for s in range(STEPS):
        if s == 0:
            arrived(inv_v, recv_sem.at[5])
        zbuf[s, z] = jnp.dot(residual.astype(BF16), inv_v[...], preferred_element_type=F32).astype(BF16)
        for i in LINE:
            remote(zbuf.at[s, z], zbuf.at[s, z], z_send.at[s], z_recv.at[s], at(dz=i)).start()
        if s == 0:
            pl.when(d == 1)(lambda: cut(1))
            forward(0)
            pass_on(history.at[0], 0)

            @pl.when(jnp.logical_and(d > 0, d < STEPS))
            def _():
                arrived(base_v.at[pl.ds(0, NX - 1)], recv_sem.at[6])

        if s == 2:
            share(0)
            loads[3].wait()
            future[0] = product(0) + take(0)
            pass_on(future.at[0], 1)

        arrived(zbuf.at[s, pl.ds(0, NZ - 1)], z_recv.at[s])
        solved = zbuf[s, 0].astype(F32)
        for i in range(1, NZ):
            solved += zbuf[s, i].astype(F32)
        current = (solved / (1.0 + beta_v[...] * solved * solved)).astype(BF16)
        c_own[s] = current
        if s < STEPS - 1:
            arrived(dl_v.at[s], recv_sem.at[3 + s])
            part = -jnp.dot(current, dl_v[0], preferred_element_type=F32)
            if s == 1:
                part -= jnp.dot(c_own[0], dl_v[1], preferred_element_type=F32)
            part += jnp.where(d == s + 1, side_by_side(base_v), 0.0)
            low, high = part[:, :256], part[:, 256:]
            pre_v[s, 0] = jnp.where(c == 0, high, low)
            remote(pre_v.at[s, 0], pre_v.at[s, 1], h_send.at[s], h_recv.at[s], at(dc=1)).start()
            arrived(pre_v.at[s, 1], h_recv.at[s])
            xbuf[s, c, y] = (jnp.where(c == 0, low, high) + pre_v[s, 1]).astype(BF16)
            for dy, dc, dx in DELAY:
                remote(xbuf.at[s, c, y], xbuf.at[s, c, y], x_send.at[s], x_recv.at[s], at(dy, dc)).start()

        landing = c_all.at[s, c, own_rows, own_columns]
        for dy, dc, dx in CORE:
            remote(c_own.at[s], landing, c_send.at[s], c_recv.at[s], at(dy, 0, 0, dx)).start()
        pltpu.make_async_copy(c_own.at[s], landing, c_recv.at[s]).start()
        if s < STEPS - 1:
            if s == 0:
                forward(1)
            arrived(mat_v.at[pl.ds(0, (ND - 1) * 32)], x_recv.at[s])
            halves = []
            for half in range(NC):
                total = xbuf[s, half, 0].astype(F32)
                for i in range(1, NY):
                    total += xbuf[s, half, i].astype(F32)
                halves.append(total)
            residual = jnp.concatenate(halves, axis=1)

    share(1)
    future[1] = product(1)
    future[1] = future[1] + take(1)
    pass_on(future.at[1], 2)

    for s in range(STEPS):
        left(zbuf.at[s, pl.ds(0, NZ - 1)], z_send.at[s])
        if s < STEPS - 1:
            left(pre_v.at[s, 0], h_send.at[s])
            left(mat_v.at[pl.ds(0, (ND - 1) * 32)], x_send.at[s])
            left(mat_v.at[pl.ds(0, (NY * NX - 1) * 32)], c_send.at[s])
            left(c_all.at[s, c], m_send.at[s])

        @pl.when(d > 0)
        def _(s=s):
            left(passed.at[s], p_send.at[s])

    left(inv_v.at[pl.ds(0, (NX - 1) * 128)], send_sem.at[2])
    left(mat_v.at[pl.ds(0, 2 * (NX - 1) * 256)], send_sem.at[4])

    @pl.when(d == 0)
    def _():
        left(mat_v.at[pl.ds(0, len(SLAB) * 16)], send_sem.at[0])

    @pl.when(d < 2)
    def _():
        left(mat_v.at[pl.ds(0, (ND - 1) * 256)], send_sem.at[1])

    @pl.when(jnp.logical_and(d > 0, d < STEPS))
    def _():
        left(base_v.at[pl.ds(0, NX - 1)], send_sem.at[3])

    share(2)
    carried[0] = product(2) + take(2)
    left(mat_v.at[pl.ds(0, (NY * NX - 1) * 32)], c_send.at[STEPS - 1])
    left(c_all.at[STEPS - 1, c], m_send.at[STEPS - 1])


def per_device(incident, onset, beta, inverse_block, delay_blocks, history_sum):
    hbm = pl.BlockSpec(memory_space=pltpu.HBM)
    vmem = pl.BlockSpec(memory_space=pltpu.VMEM)
    dma = pltpu.SemaphoreType.DMA
    steps = dma((STEPS,))
    return pl.pallas_call(
        kernel,
        out_shape=(
            pltpu.VMEM((STEPS, 64, 256), BF16),
            pltpu.VMEM((1, 64, 128), F32),
        ),
        in_specs=[hbm, pl.BlockSpec(memory_space=pltpu.SMEM), hbm, hbm, hbm, hbm],
        out_specs=(vmem, vmem),
        scratch_shapes=[
            pltpu.VMEM((64, 128), BF16),
            pltpu.VMEM((64, 128), F32),
            pltpu.VMEM((4096, 128), BF16),
            pltpu.VMEM((512, 256), BF16),
            pltpu.VMEM((2, 256, 512), BF16),
            pltpu.VMEM((2, 256, 128), BF16),
            pltpu.VMEM((1, 256), F32),
            pltpu.VMEM((NX, ROWS, 128), BF16),
            pltpu.VMEM((64, 128), F32),
            pltpu.VMEM((NX, ROWS, 128), F32),
            pltpu.VMEM((STEPS, NZ, ROWS, 256), BF16),
            pltpu.VMEM((STEPS - 1, 2, ROWS, 256), F32),
            pltpu.VMEM((STEPS - 1, NC, NY, ROWS, 256), BF16),
            pltpu.VMEM((STEPS, ROWS, 256), BF16),
            pltpu.VMEM((STEPS, NC, 64, 2048), BF16),
            pltpu.VMEM((STEPS, 64, 128), F32),
            pltpu.VMEM((STEPS - 1, 64, 128), F32),
            pltpu.VMEM((64, 128), BF16),
            dma((4,)),
            dma((5,)),
            dma((7,)),
            *[steps] * 12,
        ],
        compiler_params=pltpu.CompilerParams(
            collective_id=0, has_side_effects=True, vmem_limit_bytes=60 * 10**6
        ),
    )(incident, onset, beta.reshape(1, 256), inverse_block, delay_blocks, history_sum)


def solution(mesh):
    placed = (
        P(None, "row"),
        P(),
        P("delay"),
        P("row", "delay"),
        P("delay", None, "row"),
        P("delay", None, "row"),
    )
    return jax.shard_map(
        per_device,
        mesh=mesh,
        in_specs=placed,
        out_specs=(P(None, None, "delay"), P("delay", None, "row")),
        check_vma=False,
    )
```

```python
import jax
import jax.numpy as jnp
from jax import lax
from jax.experimental import pallas as pl
from jax.experimental.pallas import tpu as pltpu
from jax.sharding import PartitionSpec as P

STEPS = 3
MESH = pl.DeviceIdType.MESH
F32, BF16 = jnp.float32, jnp.bfloat16
NY, NC, NZ, NX = 8, 2, 8, 4
ND = NY * NC
ROWS = 16


def far_first(n):
    return sorted(range(n), key=lambda i: -min(i, n - i))


LINE = [i for i in far_first(NZ) if i]
SLAB = [(dy, dc, dx) for dy in far_first(NY) for dx in far_first(NX) for dc in range(NC) if (dy, dc, dx) != (0, 0, 0)]
SLAB.sort(key=lambda o: -min(o[0], NY - o[0]) - min(o[2], NX - o[2]))
CORE = [o for o in SLAB if o[1] == 0]
DELAY = [o for o in SLAB if o[2] == 0]
OTHER_X = [i for i in far_first(NX) if i]


def kernel(
    incident, onset, beta, inverse, matrix, history,
    currents, carried,
    onset_v, inc_v, hist_v, mat_v, inv_v, dl_v, stage_v, beta_v, first_v, res_v, base_v, zbuf, pre_v, xbuf, c_own, c_all,
    passed, future, first_src,
    load_sem, send_sem, recv_sem, z_send, z_recv, h_send, h_recv, x_send, x_recv, c_send, c_recv, m_send, m_recv,
    p_send, p_recv,
):
    d, r = lax.axis_index("delay"), lax.axis_index("row")
    y, c = d // NC, d % NC
    z, x = r // NX, r % NX

    def at(dy=0, dc=0, dz=0, dx=0):
        ty = lax.rem(y + dy, NY) if dy else y
        tc = 1 - c if dc else c
        tz = lax.rem(z + dz, NZ) if dz else z
        tx = lax.rem(x + dx, NX) if dx else x
        return (ty * NC + tc, tz * NX + tx)

    def remote(src, dst, send, recv, target):
        return pltpu.make_async_remote_copy(
            src_ref=src, dst_ref=dst, send_sem=send, recv_sem=recv, device_id=target, device_id_type=MESH
        )

    def arrived(ref, sem):
        pltpu.make_async_copy(ref, ref, sem).wait()

    left = arrived

    def rows_of(tx):
        return pl.ds(pl.multiple_of(tx * ROWS, ROWS), ROWS)

    own_rows = rows_of(x)

    loads = [
        pltpu.make_async_copy(src, dst, load_sem.at[i])
        for i, (src, dst) in enumerate(
            ((onset, onset_v), (incident, inc_v), (history.at[0], hist_v), (beta, beta_v), (matrix.at[0], mat_v))
        )
    ]
    for load in loads:
        load.start()

    barrier = pltpu.get_barrier_semaphore()
    for i in LINE:
        pl.semaphore_signal(barrier, inc=1, device_id=at(dz=i), device_id_type=MESH)
    for dy, dc, dx in SLAB:
        pl.semaphore_signal(barrier, inc=1, device_id=at(dy, dc, 0, dx), device_id_type=MESH)

    for load in loads[:4]:
        load.wait()

    @pl.when(d < STEPS)
    def _():
        row_of = lax.broadcasted_iota(jnp.int32, (8, 128), 0)
        start = []
        for i in range(0, 64, 8):
            group = jnp.zeros((8, 128), jnp.int32)
            for e in range(8):
                group = jnp.where(row_of == e, onset_v[i + e], group)
            start.append(group)
        offset = (d - jnp.concatenate(start, axis=0)).astype(F32)
        envelope = jnp.where(offset >= 0.0, jnp.exp(-((offset - 1.0) ** 2) / 4.0), 0.0)
        res_v[...] = inc_v[...].astype(F32) * envelope - hist_v[...]
        first_src[...] = res_v[...].astype(BF16)

    pl.semaphore_wait(barrier, len(LINE) + len(SLAB))


    def cut(k, half):
        for dy, dc, dx in DELAY:
            t, tr = at(dy, dc)
            rows = pl.ds(pl.multiple_of(t * 256 + half * 128, 128), 128)
            sems = send_sem.at[1], recv_sem.at[1 + 2 * k + half]
            remote(matrix.at[0, rows], stage_v.at[k, half], *sems, (t, tr)).start()
        rows = pl.ds(k * 256 + half * 128, 128)
        pltpu.make_async_copy(matrix.at[0, rows], stage_v.at[k, half], recv_sem.at[1 + 2 * k + half]).start()

    def forward(k, half):
        arrived(stage_v.at[k, half], recv_sem.at[1 + 2 * k + half])
        part = (pl.ds(half * 128, 128), pl.ds(pl.multiple_of(x * 128, 128), 128))
        for i in OTHER_X:
            remote(stage_v.at[k, half], dl_v.at[(k,) + part], send_sem.at[4], recv_sem.at[7 + k], at(dx=i)).start()
        pltpu.make_async_copy(stage_v.at[k, half], dl_v.at[(k,) + part], recv_sem.at[7 + k]).start()

    @pl.when(d == 0)
    def _():
        for dy, dc, dx in SLAB:
            t = at(dy, dc, 0, dx)
            rows = rows_of(lax.rem(x + dx, NX)) if dx else own_rows
            remote(first_src.at[rows], first_v.at[x], send_sem.at[0], recv_sem.at[0], t).start()
        pltpu.make_async_copy(first_src.at[own_rows], first_v.at[x], recv_sem.at[0]).start()
        cut(0, 0)
        cut(0, 1)

    inv_rows = pl.ds(pl.multiple_of(x * 128, 128), 128)
    for i in OTHER_X:
        remote(inverse, inv_v.at[inv_rows], send_sem.at[2], recv_sem.at[5], at(dx=i)).start()
    pltpu.make_async_copy(inverse, inv_v.at[inv_rows], recv_sem.at[5]).start()

    @pl.when(jnp.logical_and(d > 0, d < STEPS))
    def _():
        base_v[x] = res_v[own_rows]
        for i in OTHER_X:
            rows = rows_of(lax.rem(x + i, NX))
            remote(res_v.at[rows], base_v.at[x], send_sem.at[3], recv_sem.at[6], at(dx=i)).start()

    def pass_on(src, k):
        @pl.when(d > 0)
        def _():
            remote(src, passed.at[k], p_send.at[k], p_recv.at[k], (jnp.maximum(d - 1, 0), r)).start()

    def take(k):
        @pl.when(d < ND - 1)
        def _():
            arrived(passed.at[k], p_recv.at[k])

        return jnp.where(d < ND - 1, passed[k], 0.0)

    def share(s):
        arrived(c_all.at[s, c], c_recv.at[s])
        remote(c_all.at[s, c], c_all.at[s, c], m_send.at[s], m_recv.at[s], at(dc=1)).start()
        currents[s] = c_all[s, c, :, own_columns]

    own_columns = pl.ds(pl.multiple_of(y * 256, 256), 256)

    def send_values(s):
        landing = c_all.at[s, c, own_rows, own_columns]
        for dy, dc, dx in CORE:
            remote(c_own.at[s], landing, c_send.at[s], c_recv.at[s], at(dy, 0, 0, dx)).start()
        pltpu.make_async_copy(c_own.at[s], landing, c_recv.at[s]).start()

    def product(s):
        total = jnp.zeros((64, 128), F32)
        for core in (c, 1 - c):
            if core is not c:
                arrived(c_all.at[s, core], m_recv.at[s])
            values = c_all[s, core]
            for i in range(NY):
                rows = pl.ds(pl.multiple_of((NC * i + core) * 256, 256), 256)
                total += jnp.dot(values[:, i * 256 : (i + 1) * 256], mat_v[rows], preferred_element_type=F32)
        return total

    def side_by_side(blocks):
        return jnp.concatenate([blocks[i].astype(F32) for i in range(NX)], axis=1)

    arrived(first_v, recv_sem.at[0])
    residual = side_by_side(first_v)
    for s in range(STEPS):
        if s == 0:
            arrived(inv_v, recv_sem.at[5])
        zbuf[s, z] = jnp.dot(residual.astype(BF16), inv_v[...], preferred_element_type=F32).astype(BF16)
        for i in LINE:
            remote(zbuf.at[s, z], zbuf.at[s, z], z_send.at[s], z_recv.at[s], at(dz=i)).start()
        if s == 0:

            @pl.when(d == 1)
            def _():
                cut(1, 0)
                cut(1, 1)

            forward(0, 0)
            forward(0, 1)
            pass_on(history.at[0], 0)

            @pl.when(jnp.logical_and(d > 0, d < STEPS))
            def _():
                arrived(base_v.at[pl.ds(0, NX - 1)], recv_sem.at[6])

        if s == 1:
            send_values(0)
        if s == 2:
            share(0)
            loads[4].wait()
            future[0] = product(0) + take(0)
            pass_on(future.at[0], 1)

        arrived(zbuf.at[s, pl.ds(0, NZ - 1)], z_recv.at[s])
        solved = zbuf[s, 0].astype(F32)
        for i in range(1, NZ):
            solved += zbuf[s, i].astype(F32)
        current = (solved / (1.0 + beta_v[...] * solved * solved)).astype(BF16)
        c_own[s] = current
        if s < STEPS - 1:
            arrived(dl_v.at[s], recv_sem.at[7 + s])
            part = -jnp.dot(current, dl_v[0], preferred_element_type=F32)
            if s == 1:
                part -= jnp.dot(c_own[0], dl_v[1], preferred_element_type=F32)
            part += jnp.where(d == s + 1, side_by_side(base_v), 0.0)
            low, high = part[:, :256], part[:, 256:]
            pre_v[s, 0] = jnp.where(c == 0, high, low)
            remote(pre_v.at[s, 0], pre_v.at[s, 1], h_send.at[s], h_recv.at[s], at(dc=1)).start()
            arrived(pre_v.at[s, 1], h_recv.at[s])
            xbuf[s, c, y] = (jnp.where(c == 0, low, high) + pre_v[s, 1]).astype(BF16)
            for dy, dc, dx in DELAY:
                remote(xbuf.at[s, c, y], xbuf.at[s, c, y], x_send.at[s], x_recv.at[s], at(dy, dc)).start()

        if s > 0:
            send_values(s)
        if s < STEPS - 1:
            if s == 0:
                forward(1, 0)
                forward(1, 1)
            arrived(mat_v.at[pl.ds(0, (ND - 1) * 32)], x_recv.at[s])
            halves = []
            for half in range(NC):
                total = xbuf[s, half, 0].astype(F32)
                for i in range(1, NY):
                    total += xbuf[s, half, i].astype(F32)
                halves.append(total)
            residual = jnp.concatenate(halves, axis=1)

    share(1)
    future[1] = product(1)
    future[1] = future[1] + take(1)
    pass_on(future.at[1], 2)

    for s in range(STEPS):
        left(zbuf.at[s, pl.ds(0, NZ - 1)], z_send.at[s])
        if s < STEPS - 1:
            left(pre_v.at[s, 0], h_send.at[s])
            left(mat_v.at[pl.ds(0, (ND - 1) * 32)], x_send.at[s])
            left(mat_v.at[pl.ds(0, (NY * NX - 1) * 32)], c_send.at[s])
            left(c_all.at[s, c], m_send.at[s])

        @pl.when(d > 0)
        def _(s=s):
            left(passed.at[s], p_send.at[s])

    left(inv_v.at[pl.ds(0, (NX - 1) * 128)], send_sem.at[2])
    left(mat_v.at[pl.ds(0, 2 * (NX - 1) * 256)], send_sem.at[4])

    @pl.when(d == 0)
    def _():
        left(mat_v.at[pl.ds(0, len(SLAB) * 16)], send_sem.at[0])

    @pl.when(d < 2)
    def _():
        left(mat_v.at[pl.ds(0, (ND - 1) * 256)], send_sem.at[1])

    @pl.when(jnp.logical_and(d > 0, d < STEPS))
    def _():
        left(base_v.at[pl.ds(0, NX - 1)], send_sem.at[3])

    share(2)
    left(mat_v.at[pl.ds(0, (NY * NX - 1) * 32)], c_send.at[STEPS - 1])
    carried[0] = product(2) + take(2)
    left(c_all.at[STEPS - 1, c], m_send.at[STEPS - 1])


def per_device(incident, onset, beta, inverse_block, delay_blocks, history_sum):
    hbm = pl.BlockSpec(memory_space=pltpu.HBM)
    vmem = pl.BlockSpec(memory_space=pltpu.VMEM)
    dma = pltpu.SemaphoreType.DMA
    steps = dma((STEPS,))
    return pl.pallas_call(
        kernel,
        out_shape=(
            pltpu.VMEM((STEPS, 64, 256), BF16),
            pltpu.VMEM((1, 64, 128), F32),
        ),
        in_specs=[hbm] * 6,
        out_specs=(vmem, vmem),
        scratch_shapes=[
            pltpu.SMEM((64,), jnp.int32),
            pltpu.VMEM((64, 128), BF16),
            pltpu.VMEM((64, 128), F32),
            pltpu.VMEM((4096, 128), BF16),
            pltpu.VMEM((512, 256), BF16),
            pltpu.VMEM((2, 256, 512), BF16),
            pltpu.VMEM((2, 2, 128, 128), BF16),
            pltpu.VMEM((1, 256), F32),
            pltpu.VMEM((NX, ROWS, 128), BF16),
            pltpu.VMEM((64, 128), F32),
            pltpu.VMEM((NX, ROWS, 128), F32),
            pltpu.VMEM((STEPS, NZ, ROWS, 256), BF16),
            pltpu.VMEM((STEPS - 1, 2, ROWS, 256), F32),
            pltpu.VMEM((STEPS - 1, NC, NY, ROWS, 256), BF16),
            pltpu.VMEM((STEPS, ROWS, 256), BF16),
            pltpu.VMEM((STEPS, NC, 64, 2048), BF16),
            pltpu.VMEM((STEPS, 64, 128), F32),
            pltpu.VMEM((STEPS - 1, 64, 128), F32),
            pltpu.VMEM((64, 128), BF16),
            dma((5,)),
            dma((5,)),
            dma((11,)),
            *[steps] * 12,
        ],
        compiler_params=pltpu.CompilerParams(
            collective_id=0, has_side_effects=True, vmem_limit_bytes=60 * 10**6
        ),
    )(incident, onset, beta.reshape(1, 256), inverse_block, delay_blocks, history_sum)


def solution(mesh):
    placed = (
        P(None, "row"),
        P(),
        P("delay"),
        P("row", "delay"),
        P("delay", None, "row"),
        P("delay", None, "row"),
    )
    return jax.shard_map(
        per_device,
        mesh=mesh,
        in_specs=placed,
        out_specs=(P(None, None, "delay"), P("delay", None, "row")),
        check_vma=False,
    )
```

```python
import jax
import jax.numpy as jnp
from jax import lax
from jax.experimental import pallas as pl
from jax.experimental.pallas import tpu as pltpu
from jax.sharding import PartitionSpec as P

STEPS = 3
MESH = pl.DeviceIdType.MESH
F32, BF16 = jnp.float32, jnp.bfloat16
NY, NC, NZ, NX = 8, 2, 8, 4
ND = NY * NC
ROWS = 16


def far_first(n):
    return sorted(range(n), key=lambda i: -min(i, n - i))


LINE = [i for i in far_first(NZ) if i]
SLAB = [(dy, dc, dx) for dy in far_first(NY) for dx in far_first(NX) for dc in range(NC) if (dy, dc, dx) != (0, 0, 0)]
SLAB.sort(key=lambda o: -min(o[0], NY - o[0]) - min(o[2], NX - o[2]))
CORE = [o for o in SLAB if o[1] == 0]
FAR = [o for o in CORE if min(o[0], NY - o[0]) > 1]
NEAR = [o for o in CORE if o not in FAR]
FAR_SLOTS, NEAR_SLOTS = (2, 5), ((0, 2), (7, 1))
FAR_BLOCKS, NEAR_BLOCKS = 5 * NX, 3 * NX
BLOCK = 32
DELAY = [o for o in SLAB if o[2] == 0]
OTHER_X = [i for i in far_first(NX) if i]


def kernel(
    incident, onset, beta, inverse, matrix, history,
    currents, carried,
    onset_v, inc_v, hist_v, mat_v, inv_v, dl_v, stage_v, beta_v, first_v, res_v, base_v, zbuf, pre_v, xbuf, halves, c_own, c_all,
    passed, future, first_src,
    load_sem, send_sem, recv_sem, z_send, z_recv, h_send, h_recv, x_send, x_recv, c_send, c_recv, m_send, m_recv,
    p_send, p_recv, r_send, r_recv, next_sem,
):
    d, r = lax.axis_index("delay"), lax.axis_index("row")
    y, c = d // NC, d % NC
    z, x = r // NX, r % NX

    def at(dy=0, dc=0, dz=0, dx=0):
        ty = lax.rem(y + dy, NY) if dy else y
        tc = 1 - c if dc else c
        tz = lax.rem(z + dz, NZ) if dz else z
        tx = lax.rem(x + dx, NX) if dx else x
        return (ty * NC + tc, tz * NX + tx)

    def remote(src, dst, send, recv, target):
        return pltpu.make_async_remote_copy(
            src_ref=src, dst_ref=dst, send_sem=send, recv_sem=recv, device_id=target, device_id_type=MESH
        )

    def arrived(ref, sem):
        pltpu.make_async_copy(ref, ref, sem).wait()

    left = arrived

    def rows_of(tx):
        return pl.ds(pl.multiple_of(tx * ROWS, ROWS), ROWS)

    own_rows = rows_of(x)

    loads = [
        pltpu.make_async_copy(src, dst, load_sem.at[i])
        for i, (src, dst) in enumerate(
            ((onset, onset_v), (incident, inc_v), (history.at[0], hist_v), (beta, beta_v), (matrix.at[0], mat_v))
        )
    ]
    for load in loads:
        load.start()

    barrier = pltpu.get_barrier_semaphore()
    for i in LINE:
        pl.semaphore_signal(barrier, inc=1, device_id=at(dz=i), device_id_type=MESH)
    for dy, dc, dx in SLAB:
        pl.semaphore_signal(barrier, inc=1, device_id=at(dy, dc, 0, dx), device_id_type=MESH)

    for load in loads[:4]:
        load.wait()

    @pl.when(d < STEPS)
    def _():
        row_of = lax.broadcasted_iota(jnp.int32, (8, 128), 0)
        start = []
        for i in range(0, 64, 8):
            group = jnp.zeros((8, 128), jnp.int32)
            for e in range(8):
                group = jnp.where(row_of == e, onset_v[i + e], group)
            start.append(group)
        offset = (d - jnp.concatenate(start, axis=0)).astype(F32)
        envelope = jnp.where(offset >= 0.0, jnp.exp(-((offset - 1.0) ** 2) / 4.0), 0.0)
        res_v[...] = inc_v[...].astype(F32) * envelope - hist_v[...]
        first_src[...] = res_v[...].astype(BF16)

    pl.semaphore_wait(barrier, len(LINE) + len(SLAB))


    def cut(k, half):
        for dy, dc, dx in DELAY:
            t, tr = at(dy, dc)
            rows = pl.ds(pl.multiple_of(t * 256 + half * 128, 128), 128)
            sems = send_sem.at[1], recv_sem.at[1 + 2 * k + half]
            remote(matrix.at[0, rows], stage_v.at[k, half], *sems, (t, tr)).start()
        rows = pl.ds(k * 256 + half * 128, 128)
        pltpu.make_async_copy(matrix.at[0, rows], stage_v.at[k, half], recv_sem.at[1 + 2 * k + half]).start()

    def forward(k, half):
        arrived(stage_v.at[k, half], recv_sem.at[1 + 2 * k + half])
        part = (pl.ds(half * 128, 128), pl.ds(pl.multiple_of(x * 128, 128), 128))
        for i in OTHER_X:
            remote(stage_v.at[k, half], dl_v.at[(k,) + part], send_sem.at[4], recv_sem.at[7 + k], at(dx=i)).start()
        pltpu.make_async_copy(stage_v.at[k, half], dl_v.at[(k,) + part], recv_sem.at[7 + k]).start()

    @pl.when(d == 0)
    def _():
        for dy, dc, dx in SLAB:
            t = at(dy, dc, 0, dx)
            rows = rows_of(lax.rem(x + dx, NX)) if dx else own_rows
            remote(first_src.at[rows], first_v.at[x], send_sem.at[0], recv_sem.at[0], t).start()
        pltpu.make_async_copy(first_src.at[own_rows], first_v.at[x], recv_sem.at[0]).start()
        cut(0, 0)
        cut(0, 1)

    inv_rows = pl.ds(pl.multiple_of(x * 128, 128), 128)
    for i in OTHER_X:
        remote(inverse, inv_v.at[inv_rows], send_sem.at[2], recv_sem.at[5], at(dx=i)).start()
    pltpu.make_async_copy(inverse, inv_v.at[inv_rows], recv_sem.at[5]).start()

    @pl.when(jnp.logical_and(d > 0, d < STEPS))
    def _():
        base_v[x] = res_v[own_rows]
        for i in OTHER_X:
            rows = rows_of(lax.rem(x + i, NX))
            remote(res_v.at[rows], base_v.at[x], send_sem.at[3], recv_sem.at[6], at(dx=i)).start()

    def pass_on(src, k):
        @pl.when(d > 0)
        def _():
            remote(src, passed.at[k], p_send.at[k], p_recv.at[k], (jnp.maximum(d - 1, 0), r)).start()

    def take(k):
        @pl.when(d < ND - 1)
        def _():
            arrived(passed.at[k], p_recv.at[k])

        return jnp.where(d < ND - 1, passed[k], 0.0)

    def columns_of(slot, slots=1):
        return pl.ds(slot * 256, slots * 256)

    def send_values(s):
        for part, where in enumerate((FAR, NEAR)):
            for dy, dc, dx in where:
                landing = c_all.at[s, c, own_rows, columns_of((NY - dy) % NY)]
                remote(c_own.at[s], landing, c_send.at[s], c_recv.at[s, part], at(dy, 0, 0, dx)).start()
        pltpu.make_async_copy(c_own.at[s], c_all.at[s, c, own_rows, columns_of(0)], c_recv.at[s, 1]).start()

    def share(s, part):
        arrived(mat_v.at[pl.ds(0, FAR_BLOCKS * BLOCK if part == 0 else NEAR_BLOCKS * BLOCK)], c_recv.at[s, part])
        for columns in (FAR_SLOTS,) if part == 0 else NEAR_SLOTS:
            half = c_all.at[s, c, :, columns_of(*columns)]
            remote(half, half, m_send.at[s], m_recv.at[s, part], at(dc=1)).start()
        if part == 1:
            currents[s] = c_all[s, c, :, columns_of(0)]

    def multiply(s, part, core):
        total = jnp.zeros((64, 128), F32)
        for first, slots in (FAR_SLOTS,) if part == 0 else NEAR_SLOTS:
            for slot in range(first, first + slots):
                rows = pl.ds(pl.multiple_of((NC * lax.rem(y + slot, NY) + core) * 256, 256), 256)
                total += jnp.dot(c_all[s, core, :, columns_of(slot)], mat_v[rows], preferred_element_type=F32)
        return total

    def product(s):
        share(s, 0)
        total = multiply(s, 0, c)
        share(s, 1)
        total += multiply(s, 1, c)
        for part, blocks in enumerate((FAR_BLOCKS, NEAR_BLOCKS)):
            arrived(mat_v.at[pl.ds(0, blocks * BLOCK)], m_recv.at[s, part])
            total += multiply(s, part, 1 - c)
        return total

    def side_by_side(blocks):
        return jnp.concatenate([blocks[i].astype(F32) for i in range(NX)], axis=1)

    arrived(first_v, recv_sem.at[0])
    residual = jnp.concatenate([first_v[i] for i in range(NX)], axis=1)
    for s in range(STEPS):
        if s == 0:
            arrived(inv_v, recv_sem.at[5])
        zbuf[s, z] = jnp.dot(residual, inv_v[...], preferred_element_type=F32).astype(BF16)
        for i in LINE:
            remote(zbuf.at[s, z], zbuf.at[s, z], z_send.at[s], z_recv.at[s], at(dz=i)).start()
        if s == 0:
            forward(0, 0)
            forward(0, 1)

            @pl.when(d == 0)
            def _():
                left(mat_v.at[pl.ds(0, (ND - 1) * 256)], send_sem.at[1])
                pl.semaphore_signal(next_sem, inc=1, device_id=at(dc=1), device_id_type=MESH)

            @pl.when(d == 1)
            def _():
                pl.semaphore_wait(next_sem, 1)
                cut(1, 0)
                cut(1, 1)

            pass_on(history.at[0], 0)

            @pl.when(jnp.logical_and(d > 0, d < STEPS))
            def _():
                arrived(base_v.at[pl.ds(0, NX - 1)], recv_sem.at[6])

        if s == 1:
            send_values(0)
        if s == 2:
            loads[4].wait()
            future[0] = product(0) + take(0)
            pass_on(future.at[0], 1)

        arrived(zbuf.at[s, pl.ds(0, NZ - 1)], z_recv.at[s])
        solved = zbuf[s, 0].astype(F32)
        for i in range(1, NZ):
            solved += zbuf[s, i].astype(F32)
        current = (solved / (1.0 + beta_v[...] * solved * solved)).astype(BF16)
        c_own[s] = current
        if s < STEPS - 1:
            arrived(dl_v.at[s], recv_sem.at[7 + s])
            part = -jnp.dot(current, dl_v[0], preferred_element_type=F32)
            if s == 1:
                part -= jnp.dot(c_own[0], dl_v[1], preferred_element_type=F32)
            part += jnp.where(d == s + 1, side_by_side(base_v), 0.0)
            low, high = part[:, :256], part[:, 256:]
            pre_v[s, 0] = jnp.where(c == 0, high, low)
            remote(pre_v.at[s, 0], pre_v.at[s, 1], h_send.at[s], h_recv.at[s], at(dc=1)).start()
            arrived(pre_v.at[s, 1], h_recv.at[s])
            xbuf[s, y] = (jnp.where(c == 0, low, high) + pre_v[s, 1]).astype(BF16)
            for i in LINE:
                remote(xbuf.at[s, y], xbuf.at[s, y], x_send.at[s], x_recv.at[s], at(i)).start()

        if s > 0:
            send_values(s)
        if s < STEPS - 1:
            if s == 0:
                forward(1, 0)
                forward(1, 1)
            arrived(xbuf.at[s, pl.ds(0, NY - 1)], x_recv.at[s])
            total = xbuf[s, 0].astype(F32)
            for i in range(1, NY):
                total += xbuf[s, i].astype(F32)
            halves[s, c] = total.astype(BF16)
            remote(halves.at[s, c], halves.at[s, c], r_send.at[s], r_recv.at[s], at(dc=1)).start()
            arrived(halves.at[s, 1 - c], r_recv.at[s])
            residual = jnp.concatenate([halves[s, 0], halves[s, 1]], axis=1)

    future[1] = product(1)
    future[1] = future[1] + take(1)
    pass_on(future.at[1], 2)

    for s in range(STEPS):
        left(zbuf.at[s, pl.ds(0, NZ - 1)], z_send.at[s])
        if s < STEPS - 1:
            left(pre_v.at[s, 0], h_send.at[s])
            left(xbuf.at[s, pl.ds(0, NY - 1)], x_send.at[s])
            left(halves.at[s, c], r_send.at[s])
            left(mat_v.at[pl.ds(0, len(CORE) * BLOCK)], c_send.at[s])
            left(c_all.at[s, c], m_send.at[s])

        @pl.when(d > 0)
        def _(s=s):
            left(passed.at[s], p_send.at[s])

    left(inv_v.at[pl.ds(0, (NX - 1) * 128)], send_sem.at[2])
    left(mat_v.at[pl.ds(0, 2 * (NX - 1) * 256)], send_sem.at[4])

    @pl.when(d == 0)
    def _():
        left(mat_v.at[pl.ds(0, len(SLAB) * 16)], send_sem.at[0])

    @pl.when(d == 1)
    def _():
        left(mat_v.at[pl.ds(0, (ND - 1) * 256)], send_sem.at[1])

    @pl.when(jnp.logical_and(d > 0, d < STEPS))
    def _():
        left(base_v.at[pl.ds(0, NX - 1)], send_sem.at[3])

    total = product(2)
    carried[0] = total + take(2)
    left(mat_v.at[pl.ds(0, len(CORE) * BLOCK)], c_send.at[STEPS - 1])
    left(c_all.at[STEPS - 1, c], m_send.at[STEPS - 1])


def per_device(incident, onset, beta, inverse_block, delay_blocks, history_sum):
    hbm = pl.BlockSpec(memory_space=pltpu.HBM)
    vmem = pl.BlockSpec(memory_space=pltpu.VMEM)
    dma = pltpu.SemaphoreType.DMA
    steps = dma((STEPS,))
    return pl.pallas_call(
        kernel,
        out_shape=(
            pltpu.VMEM((STEPS, 64, 256), BF16),
            pltpu.VMEM((1, 64, 128), F32),
        ),
        in_specs=[hbm] * 6,
        out_specs=(vmem, vmem),
        scratch_shapes=[
            pltpu.SMEM((64,), jnp.int32),
            pltpu.VMEM((64, 128), BF16),
            pltpu.VMEM((64, 128), F32),
            pltpu.VMEM((4096, 128), BF16),
            pltpu.VMEM((512, 256), BF16),
            pltpu.VMEM((2, 256, 512), BF16),
            pltpu.VMEM((2, 2, 128, 128), BF16),
            pltpu.VMEM((1, 256), F32),
            pltpu.VMEM((NX, ROWS, 128), BF16),
            pltpu.VMEM((64, 128), F32),
            pltpu.VMEM((NX, ROWS, 128), F32),
            pltpu.VMEM((STEPS, NZ, ROWS, 256), BF16),
            pltpu.VMEM((STEPS - 1, 2, ROWS, 256), F32),
            pltpu.VMEM((STEPS - 1, NY, ROWS, 256), BF16),
            pltpu.VMEM((STEPS - 1, NC, ROWS, 256), BF16),
            pltpu.VMEM((STEPS, ROWS, 256), BF16),
            pltpu.VMEM((STEPS, NC, 64, 2048), BF16),
            pltpu.VMEM((STEPS, 64, 128), F32),
            pltpu.VMEM((STEPS - 1, 64, 128), F32),
            pltpu.VMEM((64, 128), BF16),
            dma((5,)),
            dma((5,)),
            dma((11,)),
            *[steps] * 7,
            dma((STEPS, 2)),
            steps,
            dma((STEPS, 2)),
            *[steps] * 4,
            pltpu.SemaphoreType.REGULAR,
        ],
        compiler_params=pltpu.CompilerParams(
            collective_id=0, has_side_effects=True, vmem_limit_bytes=60 * 10**6
        ),
    )(incident, onset, beta.reshape(1, 256), inverse_block, delay_blocks, history_sum)


def solution(mesh):
    placed = (
        P(None, "row"),
        P(),
        P("delay"),
        P("row", "delay"),
        P("delay", None, "row"),
        P("delay", None, "row"),
    )
    return jax.shard_map(
        per_device,
        mesh=mesh,
        in_specs=placed,
        out_specs=(P(None, None, "delay"), P("delay", None, "row")),
        check_vma=False,
    )
```

```python
import jax
import jax.numpy as jnp
from jax import lax
from jax.experimental import pallas as pl
from jax.experimental.pallas import tpu as pltpu
from jax.sharding import PartitionSpec as P

STEPS = 3
MESH = pl.DeviceIdType.MESH
F32, BF16 = jnp.float32, jnp.bfloat16
NY, NC, NZ, NX = 8, 2, 8, 4
ND = NY * NC
ROWS = 8


def far_first(n):
    return sorted(range(n), key=lambda i: -min(i, n - i))


LINE = [i for i in far_first(NZ) if i]
SLAB = [(dy, dc, dx) for dy in far_first(NY) for dx in far_first(NX) for dc in range(NC) if (dy, dc, dx) != (0, 0, 0)]
SLAB.sort(key=lambda o: -min(o[0], NY - o[0]) - min(o[2], NX - o[2]))
CORE = [o for o in SLAB if o[1] == 0]
FAR = [o for o in CORE if min(o[0], NY - o[0]) > 1]
NEAR = [o for o in CORE if o not in FAR]
FAR_SLOTS, NEAR_SLOTS = (2, 5), ((0, 2), (7, 1))
FAR_BLOCKS, NEAR_BLOCKS = 5 * NX, 3 * NX
BLOCK = 32
DELAY = [o for o in SLAB if o[2] == 0]
OTHER_X = [i for i in far_first(NX) if i]


def kernel(
    incident, onset, beta, inverse, matrix, history,
    currents, carried,
    onset_v, inc_v, hist_v, mat_v, inv_v, dl_v, stage_v, beta_v, first_v, res_v, base_v, zbuf, xbuf, c_own, c_all,
    passed, future,
    load_sem, send_sem, recv_sem, t_send, t_recv, z_send, z_recv, x_send, x_recv, c_send, c_recv, m_send, m_recv,
    p_send, p_recv, next_sem,
):
    d, r = lax.axis_index("delay"), lax.axis_index("row")
    y, c = d // NC, d % NC
    z, x = r // NX, r % NX

    def at(dy=0, dc=0, dz=0, dx=0):
        ty = lax.rem(y + dy, NY) if dy else y
        tc = 1 - c if dc else c
        tz = lax.rem(z + dz, NZ) if dz else z
        tx = lax.rem(x + dx, NX) if dx else x
        return (ty * NC + tc, tz * NX + tx)

    def remote(src, dst, send, recv, target):
        return pltpu.make_async_remote_copy(
            src_ref=src, dst_ref=dst, send_sem=send, recv_sem=recv, device_id=target, device_id_type=MESH
        )

    def arrived(ref, sem):
        pltpu.make_async_copy(ref, ref, sem).wait()

    left = arrived

    def rows_of(dx, dc):
        t = (lax.rem(x + dx, NX) if dx else x) * NC + (1 - c if dc else c)
        return pl.ds(pl.multiple_of(t * ROWS, ROWS), ROWS)

    own_rows = rows_of(0, 0)

    def stacked(wide):
        return jnp.concatenate([wide[:, :256], wide[:, 256:]], axis=0)

    def unstacked(tall):
        return jnp.concatenate([tall[:ROWS], tall[ROWS:]], axis=1)

    def halves(block):
        block = block.astype(F32).reshape(NX, NC, ROWS, 256)
        return block[:, 0].reshape(NX * ROWS, 256), block[:, 1].reshape(NX * ROWS, 256)

    def in_order(zeroth, first, width):
        parts = [v.reshape(NX, 1, ROWS, width) for v in (zeroth, first)]
        return jnp.concatenate(parts, axis=1).reshape(64, width)

    loads = [
        pltpu.make_async_copy(src, dst, load_sem.at[i])
        for i, (src, dst) in enumerate(
            ((onset, onset_v), (incident, inc_v), (history.at[0], hist_v), (beta, beta_v.at[c]), (matrix.at[0], mat_v))
        )
    ]
    for load in loads:
        load.start()

    barrier = pltpu.get_barrier_semaphore()
    for i in LINE:
        pl.semaphore_signal(barrier, inc=1, device_id=at(dz=i), device_id_type=MESH)
    for dy, dc, dx in SLAB:
        pl.semaphore_signal(barrier, inc=1, device_id=at(dy, dc, 0, dx), device_id_type=MESH)

    for load in loads[:4]:
        load.wait()

    @pl.when(d < STEPS)
    def _():
        row_of = lax.broadcasted_iota(jnp.int32, (8, 128), 0)
        start = []
        for i in range(0, 64, 8):
            group = jnp.zeros((8, 128), jnp.int32)
            for e in range(8):
                group = jnp.where(row_of == e, onset_v[i + e], group)
            start.append(group)
        offset = (d - jnp.concatenate(start, axis=0)).astype(F32)
        envelope = jnp.where(offset >= 0.0, jnp.exp(-((offset - 1.0) ** 2) / 4.0), 0.0)
        res_v[...] = inc_v[...].astype(F32) * envelope - hist_v[...]

    pl.semaphore_wait(barrier, len(LINE) + len(SLAB))


    def cut(k, half):
        for dy, dc, dx in DELAY:
            t, tr = at(dy, dc)
            rows = pl.ds(pl.multiple_of(t * 256 + half * 128, 128), 128)
            sems = send_sem.at[1], recv_sem.at[1 + 2 * k + half]
            remote(matrix.at[0, rows], stage_v.at[k, half], *sems, (t, tr)).start()
        rows = pl.ds(k * 256 + half * 128, 128)
        pltpu.make_async_copy(matrix.at[0, rows], stage_v.at[k, half], recv_sem.at[1 + 2 * k + half]).start()

    def forward(k, half):
        arrived(stage_v.at[k, half], recv_sem.at[1 + 2 * k + half])
        rows = pl.ds(pl.multiple_of(c * 256 + half * 128, 128), 128)
        landing = dl_v.at[k, rows, pl.ds(pl.multiple_of(x * 128, 128), 128)]
        for i in OTHER_X:
            remote(stage_v.at[k, half], landing, send_sem.at[4], recv_sem.at[7 + 2 * k + half], at(dx=i)).start()
        pltpu.make_async_copy(stage_v.at[k, half], landing, recv_sem.at[7 + 2 * k + half]).start()

    def to_mate(ref, i):
        remote(ref, ref, t_send.at[i], t_recv.at[i], at(dc=1)).start()

    def share_matrix(k):
        for half in range(2):
            rows = pl.ds(pl.multiple_of(c * 256 + half * 128, 128), 128)
            arrived(dl_v.at[k, rows], recv_sem.at[7 + 2 * k + half])
            to_mate(dl_v.at[k, rows], 2 + 2 * k + half)

    def have_matrix(k):
        for half in range(2):
            arrived(dl_v.at[k, pl.ds(0, 128)], t_recv.at[2 + 2 * k + half])

    to_mate(beta_v.at[c], 1)

    @pl.when(d == 0)
    def _():
        for dy, dc, dx in SLAB:
            t = at(dy, dc, 0, dx)
            remote(res_v.at[rows_of(dx, dc)], first_v.at[x], send_sem.at[0], recv_sem.at[0], t).start()
        pltpu.make_async_copy(res_v.at[own_rows], first_v.at[x], recv_sem.at[0]).start()
        cut(0, 0)
        cut(0, 1)

    inv_columns = pl.ds(pl.multiple_of(c * 256, 256), 256)
    inv_landing = inv_v.at[pl.ds(pl.multiple_of(x * 128, 128), 128), inv_columns]
    for i in OTHER_X:
        remote(inverse, inv_landing, send_sem.at[2], recv_sem.at[5], at(dx=i)).start()
    pltpu.make_async_copy(inverse, inv_landing, recv_sem.at[5]).start()

    @pl.when(jnp.logical_and(d > 0, d < STEPS))
    def _():
        for dy, dc, dx in SLAB:
            if dy == 0:
                remote(res_v.at[rows_of(dx, dc)], base_v.at[x], send_sem.at[3], recv_sem.at[6], at(0, dc, 0, dx)).start()
        pltpu.make_async_copy(res_v.at[own_rows], base_v.at[x], recv_sem.at[6]).start()

    def pass_on(src, k):
        @pl.when(d > 0)
        def _():
            remote(src, passed.at[k], p_send.at[k], p_recv.at[k], (jnp.maximum(d - 1, 0), r)).start()

    def take(k):
        @pl.when(d < ND - 1)
        def _():
            arrived(passed.at[k], p_recv.at[k])

        return jnp.where(d < ND - 1, passed[k], 0.0)

    slot_rows = pl.ds(pl.multiple_of(x * NC * ROWS, NC * ROWS), NC * ROWS)

    def send_values(s):
        for part, where in enumerate((FAR, NEAR)):
            for dy, dc, dx in where:
                landing = c_all.at[s, c, (NY - dy) % NY, slot_rows]
                remote(c_own.at[s], landing, c_send.at[s], c_recv.at[s, part], at(dy, 0, 0, dx)).start()
        pltpu.make_async_copy(c_own.at[s], c_all.at[s, c, 0, slot_rows], c_recv.at[s, 1]).start()

    def share(s, part):
        arrived(mat_v.at[pl.ds(0, FAR_BLOCKS * BLOCK if part == 0 else NEAR_BLOCKS * BLOCK)], c_recv.at[s, part])
        for slots in (FAR_SLOTS,) if part == 0 else NEAR_SLOTS:
            piece = c_all.at[s, c, pl.ds(*slots)]
            remote(piece, piece, m_send.at[s], m_recv.at[s, part], at(dc=1)).start()

    def multiply(s, part, core):
        total = jnp.zeros((NX * ROWS, 128), F32)
        for first, slots in (FAR_SLOTS,) if part == 0 else NEAR_SLOTS:
            for slot in range(first, first + slots):
                for half, values in enumerate(halves(c_all[s, core, slot])):
                    at_row = (NC * lax.rem(y + slot, NY) + half) * 256
                    rows = pl.ds(pl.multiple_of(at_row, 256), 256)
                    total += jnp.dot(values.astype(BF16), mat_v[rows], preferred_element_type=F32)
        return total

    def product(s):
        share(s, 0)
        own = multiply(s, 0, c)
        share(s, 1)
        own += multiply(s, 1, c)
        other = jnp.zeros((NX * ROWS, 128), F32)
        for part, blocks in enumerate((FAR_BLOCKS, NEAR_BLOCKS)):
            arrived(mat_v.at[pl.ds(0, blocks * BLOCK)], m_recv.at[s, part])
            other += multiply(s, part, 1 - c)
        columns = [jnp.where(c == 0, *halves(c_all[s, core, 0])) for core in range(NC)]
        currents[s] = in_order(*columns, 256).astype(BF16)
        return in_order(jnp.where(c == 0, own, other), jnp.where(c == 0, other, own), 128)

    def side_by_side(blocks):
        return jnp.concatenate([blocks[i].astype(F32) for i in range(NX)], axis=1)

    arrived(inv_v.at[:, inv_columns], recv_sem.at[5])
    to_mate(inv_v.at[:, inv_columns], 0)
    arrived(first_v, recv_sem.at[0])
    residual = side_by_side(first_v)
    for s in range(STEPS):
        if s == 0:
            arrived(inv_v.at[:, inv_columns], t_recv.at[0])
        partial_sum = jnp.dot(residual.astype(BF16), inv_v[...], preferred_element_type=F32)
        zbuf[s, z] = stacked(partial_sum).astype(BF16)
        for i in LINE:
            remote(zbuf.at[s, z], zbuf.at[s, z], z_send.at[s], z_recv.at[s], at(dz=i)).start()
        if s == 0:
            forward(0, 0)
            forward(0, 1)

            @pl.when(d == 0)
            def _():
                left(mat_v.at[pl.ds(0, (ND - 1) * 256)], send_sem.at[1])
                pl.semaphore_signal(next_sem, inc=1, device_id=at(dc=1), device_id_type=MESH)

            @pl.when(d == 1)
            def _():
                pl.semaphore_wait(next_sem, 1)
                cut(1, 0)
                cut(1, 1)

            pass_on(history.at[0], 0)

            @pl.when(y < STEPS - 1)
            def _():
                arrived(base_v, recv_sem.at[6])

            arrived(beta_v.at[c], t_recv.at[1])
            beta_wide = jnp.concatenate([jnp.broadcast_to(beta_v[i], (ROWS, 256)) for i in range(NC)], axis=0)

        if s == 1:
            share_matrix(1)
            send_values(0)
        if s == 2:
            loads[4].wait()
            future[0] = product(0) + take(0)
            pass_on(future.at[0], 1)

        arrived(zbuf.at[s, pl.ds(0, NZ - 1)], z_recv.at[s])
        solved = zbuf[s, 0].astype(F32)
        for i in range(1, NZ):
            solved += zbuf[s, i].astype(F32)
        current = (solved / (1.0 + beta_wide * solved * solved)).astype(BF16)
        c_own[s] = current
        if s < STEPS - 1:
            if s == 0:
                share_matrix(0)
            have_matrix(s)
            wide = unstacked(current.astype(F32)).astype(BF16)
            part = -jnp.dot(wide, dl_v[0], preferred_element_type=F32)
            if s == 0:
                earlier = wide
            else:
                part -= jnp.dot(earlier, dl_v[1], preferred_element_type=F32)
            part += jnp.where(y == s, side_by_side(base_v), 0.0)
            xbuf[s, y] = stacked(part).astype(BF16)
            for i in LINE:
                remote(xbuf.at[s, y], xbuf.at[s, y], x_send.at[s], x_recv.at[s], at(i)).start()

        if s > 0:
            send_values(s)
        if s < STEPS - 1:
            if s == 0:
                forward(1, 0)
                forward(1, 1)
            arrived(xbuf.at[s, pl.ds(0, NY - 1)], x_recv.at[s])
            total = xbuf[s, 0].astype(F32)
            for i in range(1, NY):
                total += xbuf[s, i].astype(F32)
            residual = unstacked(total)

    future[1] = product(1)
    future[1] = future[1] + take(1)
    pass_on(future.at[1], 2)

    for s in range(STEPS):
        left(zbuf.at[s, pl.ds(0, NZ - 1)], z_send.at[s])
        if s < STEPS - 1:
            left(xbuf.at[s, pl.ds(0, NY - 1)], x_send.at[s])
            left(mat_v.at[pl.ds(0, len(CORE) * BLOCK)], c_send.at[s])
            left(c_all.at[s, c], m_send.at[s])

        @pl.when(d > 0)
        def _(s=s):
            left(passed.at[s], p_send.at[s])

    left(inv_v.at[pl.ds(0, (NX - 1) * 128), inv_columns], send_sem.at[2])
    left(inv_v.at[:, inv_columns], t_send.at[0])
    left(beta_v.at[c], t_send.at[1])
    for i in range(2, 6):
        left(dl_v.at[0, pl.ds(0, 128)], t_send.at[i])
    left(mat_v.at[pl.ds(0, 2 * (NX - 1) * 256)], send_sem.at[4])

    @pl.when(d == 0)
    def _():
        left(mat_v.at[pl.ds(0, len(SLAB) * 16)], send_sem.at[0])

    @pl.when(d == 1)
    def _():
        left(mat_v.at[pl.ds(0, (ND - 1) * 256)], send_sem.at[1])

    @pl.when(jnp.logical_and(d > 0, d < STEPS))
    def _():
        left(mat_v.at[pl.ds(0, (NX * NC - 1) * 16)], send_sem.at[3])

    total = product(2)
    carried[0] = total + take(2)
    left(mat_v.at[pl.ds(0, len(CORE) * BLOCK)], c_send.at[STEPS - 1])
    left(c_all.at[STEPS - 1, c], m_send.at[STEPS - 1])


def per_device(incident, onset, beta, inverse_block, delay_blocks, history_sum):
    hbm = pl.BlockSpec(memory_space=pltpu.HBM)
    vmem = pl.BlockSpec(memory_space=pltpu.VMEM)
    dma = pltpu.SemaphoreType.DMA
    steps = dma((STEPS,))
    return pl.pallas_call(
        kernel,
        out_shape=(
            pltpu.VMEM((STEPS, 64, 256), BF16),
            pltpu.VMEM((1, 64, 128), F32),
        ),
        in_specs=[hbm] * 6,
        out_specs=(vmem, vmem),
        scratch_shapes=[
            pltpu.SMEM((64,), jnp.int32),
            pltpu.VMEM((64, 128), BF16),
            pltpu.VMEM((64, 128), F32),
            pltpu.VMEM((4096, 128), BF16),
            pltpu.VMEM((512, 512), BF16),
            pltpu.VMEM((2, 512, 512), BF16),
            pltpu.VMEM((2, 2, 128, 128), BF16),
            pltpu.VMEM((NC, 1, 256), F32),
            pltpu.VMEM((NX, ROWS, 128), F32),
            pltpu.VMEM((64, 128), F32),
            pltpu.VMEM((NX, ROWS, 128), F32),
            pltpu.VMEM((STEPS, NZ, 16, 256), BF16),
            pltpu.VMEM((STEPS - 1, NY, 16, 256), BF16),
            pltpu.VMEM((STEPS, 16, 256), BF16),
            pltpu.VMEM((STEPS, NC, NY, 64, 256), BF16),
            pltpu.VMEM((STEPS, 64, 128), F32),
            pltpu.VMEM((STEPS - 1, 64, 128), F32),
            dma((5,)),
            dma((5,)),
            dma((11,)),
            dma((6,)),
            dma((6,)),
            *[steps] * 5,
            dma((STEPS, 2)),
            steps,
            dma((STEPS, 2)),
            *[steps] * 2,
            pltpu.SemaphoreType.REGULAR,
        ],
        compiler_params=pltpu.CompilerParams(
            collective_id=0, has_side_effects=True, vmem_limit_bytes=60 * 10**6
        ),
    )(incident, onset, beta.reshape(1, 256), inverse_block, delay_blocks, history_sum)


def solution(mesh):
    placed = (
        P(None, "row"),
        P(),
        P("delay"),
        P("row", "delay"),
        P("delay", None, "row"),
        P("delay", None, "row"),
    )
    return jax.shard_map(
        per_device,
        mesh=mesh,
        in_specs=placed,
        out_specs=(P(None, None, "delay"), P("delay", None, "row")),
        check_vma=False,
    )
```

```python
import jax
import jax.numpy as jnp
from jax import lax
from jax.experimental import pallas as pl
from jax.experimental.pallas import tpu as pltpu
from jax.sharding import PartitionSpec as P

STEPS = 3
MESH = pl.DeviceIdType.MESH
F32, BF16 = jnp.float32, jnp.bfloat16
NY, NC, NZ, NX = 8, 2, 8, 4
ND = NY * NC
ROWS = 8


def far_first(n):
    return sorted(range(n), key=lambda i: -min(i, n - i))


LINE = [i for i in far_first(NZ) if i]
SLAB = [(dy, dc, dx) for dy in far_first(NY) for dx in far_first(NX) for dc in range(NC) if (dy, dc, dx) != (0, 0, 0)]
SLAB.sort(key=lambda o: -min(o[0], NY - o[0]) - min(o[2], NX - o[2]))
CORE = [o for o in SLAB if o[1] == 0]
FAR = [o for o in CORE if min(o[0], NY - o[0]) > 1]
NEAR = [o for o in CORE if o not in FAR]
FAR_SLOTS, NEAR_SLOTS = (2, 5), ((0, 2), (7, 1))
FAR_BLOCKS, NEAR_BLOCKS = 5 * NX, 3 * NX
BLOCK = 32
DELAY = [o for o in SLAB if o[2] == 0]
OTHER_X = [i for i in far_first(NX) if i]


def kernel(
    incident, onset, beta, inverse, matrix, history,
    currents, carried,
    onset_v, inc_v, hist_v, mat_v, inv_v, dl_v, stage_v, beta_v, first_v, res_v, base_v, zbuf, xbuf, c_own, c_all,
    passed, future,
    load_sem, send_sem, recv_sem, t_send, t_recv, z_send, z_recv, x_send, x_recv, c_send, c_recv, m_send, m_recv,
    p_send, p_recv, next_sem,
):
    d, r = lax.axis_index("delay"), lax.axis_index("row")
    y, c = d // NC, d % NC
    z, x = r // NX, r % NX

    def at(dy=0, dc=0, dz=0, dx=0):
        ty = lax.rem(y + dy, NY) if dy else y
        tc = 1 - c if dc else c
        tz = lax.rem(z + dz, NZ) if dz else z
        tx = lax.rem(x + dx, NX) if dx else x
        return (ty * NC + tc, tz * NX + tx)

    def remote(src, dst, send, recv, target):
        return pltpu.make_async_remote_copy(
            src_ref=src, dst_ref=dst, send_sem=send, recv_sem=recv, device_id=target, device_id_type=MESH
        )

    def arrived(ref, sem):
        pltpu.make_async_copy(ref, ref, sem).wait()

    left = arrived

    def rows_of(dx, dc):
        t = (lax.rem(x + dx, NX) if dx else x) * NC + (1 - c if dc else c)
        return pl.ds(pl.multiple_of(t * ROWS, ROWS), ROWS)

    own_rows = rows_of(0, 0)

    def stacked(wide):
        return jnp.concatenate([wide[:, :256], wide[:, 256:]], axis=0)

    def unstacked(tall):
        return jnp.concatenate([tall[:ROWS], tall[ROWS:]], axis=1)

    def halves(block):
        block = block.astype(F32).reshape(NX, NC, ROWS, 256)
        return block[:, 0].reshape(NX * ROWS, 256), block[:, 1].reshape(NX * ROWS, 256)

    def in_order(zeroth, first, width):
        parts = [v.reshape(NX, 1, ROWS, width) for v in (zeroth, first)]
        return jnp.concatenate(parts, axis=1).reshape(64, width)

    loads = [
        pltpu.make_async_copy(src, dst, load_sem.at[i])
        for i, (src, dst) in enumerate(
            ((onset, onset_v), (incident, inc_v), (history.at[0], hist_v), (beta, beta_v.at[c]), (matrix.at[0], mat_v))
        )
    ]
    for load in loads:
        load.start()

    barrier = pltpu.get_barrier_semaphore()
    for i in LINE:
        pl.semaphore_signal(barrier, inc=1, device_id=at(dz=i), device_id_type=MESH)
    for dy, dc, dx in SLAB:
        pl.semaphore_signal(barrier, inc=1, device_id=at(dy, dc, 0, dx), device_id_type=MESH)

    for load in loads[:4]:
        load.wait()

    @pl.when(d < STEPS)
    def _():
        row_of = lax.broadcasted_iota(jnp.int32, (8, 128), 0)
        start = []
        for i in range(0, 64, 8):
            group = jnp.zeros((8, 128), jnp.int32)
            for e in range(8):
                group = jnp.where(row_of == e, onset_v[i + e], group)
            start.append(group)
        offset = (d - jnp.concatenate(start, axis=0)).astype(F32)
        envelope = jnp.where(offset >= 0.0, jnp.exp(-((offset - 1.0) ** 2) / 4.0), 0.0)
        res_v[...] = inc_v[...].astype(F32) * envelope - hist_v[...]

    pl.semaphore_wait(barrier, len(LINE) + len(SLAB))


    def cut(k, half):
        for dy, dc, dx in DELAY:
            t, tr = at(dy, dc)
            rows = pl.ds(pl.multiple_of(t * 256 + half * 128, 128), 128)
            sems = send_sem.at[1], recv_sem.at[1 + 2 * k + half]
            remote(matrix.at[0, rows], stage_v.at[k, half], *sems, (t, tr)).start()
        rows = pl.ds(k * 256 + half * 128, 128)
        pltpu.make_async_copy(matrix.at[0, rows], stage_v.at[k, half], recv_sem.at[1 + 2 * k + half]).start()

    def forward(k, half):
        arrived(stage_v.at[k, half], recv_sem.at[1 + 2 * k + half])
        rows = pl.ds(pl.multiple_of(c * 256 + half * 128, 128), 128)
        landing = dl_v.at[k, rows, pl.ds(pl.multiple_of(x * 128, 128), 128)]
        for i in OTHER_X:
            remote(stage_v.at[k, half], landing, send_sem.at[4], recv_sem.at[7 + 2 * k + half], at(dx=i)).start()
        pltpu.make_async_copy(stage_v.at[k, half], landing, recv_sem.at[7 + 2 * k + half]).start()

    def to_mate(ref, i):
        remote(ref, ref, t_send.at[i], t_recv.at[i], at(dc=1)).start()

    def share_matrix(k):
        for half in range(2):
            rows = pl.ds(pl.multiple_of(c * 256 + half * 128, 128), 128)
            arrived(dl_v.at[k, rows], recv_sem.at[7 + 2 * k + half])
            to_mate(dl_v.at[k, rows], 2 + 2 * k + half)

    def have_matrix(k):
        for half in range(2):
            arrived(dl_v.at[k, pl.ds(0, 128)], t_recv.at[2 + 2 * k + half])

    to_mate(beta_v.at[c], 1)

    @pl.when(d == 0)
    def _():
        for dy, dc, dx in SLAB:
            t = at(dy, dc, 0, dx)
            remote(res_v.at[rows_of(dx, dc)], first_v.at[x], send_sem.at[0], recv_sem.at[0], t).start()
        pltpu.make_async_copy(res_v.at[own_rows], first_v.at[x], recv_sem.at[0]).start()
        cut(0, 0)
        cut(0, 1)

    inv_columns = pl.ds(pl.multiple_of(c * 256, 256), 256)
    inv_landing = inv_v.at[pl.ds(pl.multiple_of(x * 128, 128), 128), inv_columns]
    for i in OTHER_X:
        remote(inverse, inv_landing, send_sem.at[2], recv_sem.at[5], at(dx=i)).start()
    pltpu.make_async_copy(inverse, inv_landing, recv_sem.at[5]).start()

    @pl.when(jnp.logical_and(d > 0, d < STEPS))
    def _():
        for dy, dc, dx in SLAB:
            if dy == 0:
                remote(res_v.at[rows_of(dx, dc)], base_v.at[x], send_sem.at[3], recv_sem.at[6], at(0, dc, 0, dx)).start()
        pltpu.make_async_copy(res_v.at[own_rows], base_v.at[x], recv_sem.at[6]).start()

    def pass_on(src, k):
        @pl.when(d > 0)
        def _():
            remote(src, passed.at[k], p_send.at[k], p_recv.at[k], (jnp.maximum(d - 1, 0), r)).start()

    def take(k):
        @pl.when(d < ND - 1)
        def _():
            arrived(passed.at[k], p_recv.at[k])

        return jnp.where(d < ND - 1, passed[k], 0.0)

    slot_rows = pl.ds(pl.multiple_of(x * NC * ROWS, NC * ROWS), NC * ROWS)

    def send_values(s):
        for part, where in enumerate((FAR, NEAR)):
            for dy, dc, dx in where:
                landing = c_all.at[s, c, (NY - dy) % NY, slot_rows]
                remote(c_own.at[s], landing, c_send.at[s], c_recv.at[s, part], at(dy, 0, 0, dx)).start()
        pltpu.make_async_copy(c_own.at[s], c_all.at[s, c, 0, slot_rows], c_recv.at[s, 1]).start()

    def share(s, part):
        arrived(mat_v.at[pl.ds(0, FAR_BLOCKS * BLOCK if part == 0 else NEAR_BLOCKS * BLOCK)], c_recv.at[s, part])
        for slots in (FAR_SLOTS,) if part == 0 else NEAR_SLOTS:
            piece = c_all.at[s, c, pl.ds(*slots)]
            remote(piece, piece, m_send.at[s], m_recv.at[s, part], at(dc=1)).start()

    def multiply(s, part, core):
        total = jnp.zeros((NX * ROWS, 128), F32)
        for first, slots in (FAR_SLOTS,) if part == 0 else NEAR_SLOTS:
            for slot in range(first, first + slots):
                for half, values in enumerate(halves(c_all[s, core, slot])):
                    at_row = (NC * lax.rem(y + slot, NY) + half) * 256
                    rows = pl.ds(pl.multiple_of(at_row, 256), 256)
                    total += jnp.dot(values.astype(BF16), mat_v[rows], preferred_element_type=F32)
        return total

    def product(s):
        share(s, 0)
        own = multiply(s, 0, c)
        share(s, 1)
        own += multiply(s, 1, c)
        other = jnp.zeros((NX * ROWS, 128), F32)
        for part, blocks in enumerate((FAR_BLOCKS, NEAR_BLOCKS)):
            arrived(mat_v.at[pl.ds(0, blocks * BLOCK)], m_recv.at[s, part])
            other += multiply(s, part, 1 - c)
        columns = [jnp.where(c == 0, *halves(c_all[s, core, 0])) for core in range(NC)]
        currents[s] = in_order(*columns, 256).astype(BF16)
        return in_order(jnp.where(c == 0, own, other), jnp.where(c == 0, other, own), 128)

    def side_by_side(blocks):
        return jnp.concatenate([blocks[i].astype(F32) for i in range(NX)], axis=1)

    arrived(inv_v.at[:, inv_columns], recv_sem.at[5])
    to_mate(inv_v.at[:, inv_columns], 0)
    arrived(first_v, recv_sem.at[0])
    residual = side_by_side(first_v)
    for s in range(STEPS):
        if s == 0:
            arrived(inv_v.at[:, inv_columns], t_recv.at[0])
        partial_sum = jnp.dot(residual.astype(BF16), inv_v[...], preferred_element_type=F32)
        zbuf[s, z] = stacked(partial_sum).astype(BF16)
        for i in LINE:
            remote(zbuf.at[s, z], zbuf.at[s, z], z_send.at[s], z_recv.at[s], at(dz=i)).start()
        if s == 0:
            forward(0, 0)
            forward(0, 1)

            @pl.when(d == 0)
            def _():
                left(mat_v.at[pl.ds(0, (ND - 1) * 256)], send_sem.at[1])
                pl.semaphore_signal(next_sem, inc=1, device_id=at(dc=1), device_id_type=MESH)

            @pl.when(d == 1)
            def _():
                pl.semaphore_wait(next_sem, 1)
                cut(1, 0)
                cut(1, 1)

            pass_on(history.at[0], 0)

            @pl.when(y < STEPS - 1)
            def _():
                arrived(base_v, recv_sem.at[6])

            arrived(beta_v.at[c], t_recv.at[1])
            share_matrix(0)
            beta_wide = jnp.concatenate([jnp.broadcast_to(beta_v[i], (ROWS, 256)) for i in range(NC)], axis=0)

        if s == 1:
            send_values(0)
            share_matrix(1)
        if s == 2:
            send_values(1)
            loads[4].wait()
            future[0] = product(0) + take(0)
            pass_on(future.at[0], 1)

        arrived(zbuf.at[s, pl.ds(0, NZ - 1)], z_recv.at[s])
        solved = zbuf[s, 0].astype(F32)
        for i in range(1, NZ):
            solved += zbuf[s, i].astype(F32)
        current = (solved / (1.0 + beta_wide * solved * solved)).astype(BF16)
        c_own[s] = current
        if s < STEPS - 1:
            have_matrix(s)
            wide = unstacked(current.astype(F32)).astype(BF16)
            part = -jnp.dot(wide, dl_v[0], preferred_element_type=F32)
            if s == 0:
                earlier = wide
            else:
                part -= jnp.dot(earlier, dl_v[1], preferred_element_type=F32)
            part += jnp.where(y == s, side_by_side(base_v), 0.0)
            xbuf[s, y] = stacked(part).astype(BF16)
            for i in LINE:
                remote(xbuf.at[s, y], xbuf.at[s, y], x_send.at[s], x_recv.at[s], at(i)).start()

        if s == STEPS - 1:
            send_values(s)
        if s < STEPS - 1:
            if s == 0:
                forward(1, 0)
                forward(1, 1)
            arrived(xbuf.at[s, pl.ds(0, NY - 1)], x_recv.at[s])
            total = xbuf[s, 0].astype(F32)
            for i in range(1, NY):
                total += xbuf[s, i].astype(F32)
            residual = unstacked(total)

    future[1] = product(1)
    future[1] = future[1] + take(1)
    pass_on(future.at[1], 2)

    for s in range(STEPS):
        left(zbuf.at[s, pl.ds(0, NZ - 1)], z_send.at[s])
        if s < STEPS - 1:
            left(xbuf.at[s, pl.ds(0, NY - 1)], x_send.at[s])
            left(mat_v.at[pl.ds(0, len(CORE) * BLOCK)], c_send.at[s])
            left(c_all.at[s, c], m_send.at[s])

        @pl.when(d > 0)
        def _(s=s):
            left(passed.at[s], p_send.at[s])

    left(inv_v.at[pl.ds(0, (NX - 1) * 128), inv_columns], send_sem.at[2])
    left(inv_v.at[:, inv_columns], t_send.at[0])
    left(beta_v.at[c], t_send.at[1])
    for i in range(2, 6):
        left(dl_v.at[0, pl.ds(0, 128)], t_send.at[i])
    left(mat_v.at[pl.ds(0, 2 * (NX - 1) * 256)], send_sem.at[4])

    @pl.when(d == 0)
    def _():
        left(mat_v.at[pl.ds(0, len(SLAB) * 16)], send_sem.at[0])

    @pl.when(d == 1)
    def _():
        left(mat_v.at[pl.ds(0, (ND - 1) * 256)], send_sem.at[1])

    @pl.when(jnp.logical_and(d > 0, d < STEPS))
    def _():
        left(mat_v.at[pl.ds(0, (NX * NC - 1) * 16)], send_sem.at[3])

    total = product(2)
    carried[0] = total + take(2)
    left(mat_v.at[pl.ds(0, len(CORE) * BLOCK)], c_send.at[STEPS - 1])
    left(c_all.at[STEPS - 1, c], m_send.at[STEPS - 1])


def per_device(incident, onset, beta, inverse_block, delay_blocks, history_sum):
    hbm = pl.BlockSpec(memory_space=pltpu.HBM)
    vmem = pl.BlockSpec(memory_space=pltpu.VMEM)
    dma = pltpu.SemaphoreType.DMA
    steps = dma((STEPS,))
    return pl.pallas_call(
        kernel,
        out_shape=(
            pltpu.VMEM((STEPS, 64, 256), BF16),
            pltpu.VMEM((1, 64, 128), F32),
        ),
        in_specs=[hbm] * 6,
        out_specs=(vmem, vmem),
        scratch_shapes=[
            pltpu.SMEM((64,), jnp.int32),
            pltpu.VMEM((64, 128), BF16),
            pltpu.VMEM((64, 128), F32),
            pltpu.VMEM((4096, 128), BF16),
            pltpu.VMEM((512, 512), BF16),
            pltpu.VMEM((2, 512, 512), BF16),
            pltpu.VMEM((2, 2, 128, 128), BF16),
            pltpu.VMEM((NC, 1, 256), F32),
            pltpu.VMEM((NX, ROWS, 128), F32),
            pltpu.VMEM((64, 128), F32),
            pltpu.VMEM((NX, ROWS, 128), F32),
            pltpu.VMEM((STEPS, NZ, 16, 256), BF16),
            pltpu.VMEM((STEPS - 1, NY, 16, 256), BF16),
            pltpu.VMEM((STEPS, 16, 256), BF16),
            pltpu.VMEM((STEPS, NC, NY, 64, 256), BF16),
            pltpu.VMEM((STEPS, 64, 128), F32),
            pltpu.VMEM((STEPS - 1, 64, 128), F32),
            dma((5,)),
            dma((5,)),
            dma((11,)),
            dma((6,)),
            dma((6,)),
            *[steps] * 5,
            dma((STEPS, 2)),
            steps,
            dma((STEPS, 2)),
            *[steps] * 2,
            pltpu.SemaphoreType.REGULAR,
        ],
        compiler_params=pltpu.CompilerParams(
            collective_id=0, has_side_effects=True, vmem_limit_bytes=60 * 10**6
        ),
    )(incident, onset, beta.reshape(1, 256), inverse_block, delay_blocks, history_sum)


def solution(mesh):
    placed = (
        P(None, "row"),
        P(),
        P("delay"),
        P("row", "delay"),
        P("delay", None, "row"),
        P("delay", None, "row"),
    )
    return jax.shard_map(
        per_device,
        mesh=mesh,
        in_specs=placed,
        out_specs=(P(None, None, "delay"), P("delay", None, "row")),
        check_vma=False,
    )
```

```python
import jax
import jax.numpy as jnp
from jax import lax
from jax.experimental import pallas as pl
from jax.experimental.pallas import tpu as pltpu
from jax.sharding import PartitionSpec as P

STEPS = 3
MESH = pl.DeviceIdType.MESH
F32, BF16 = jnp.float32, jnp.bfloat16
NY, NC, NZ, NX = 8, 2, 8, 4
ND = NY * NC
ROWS = 8


def far_first(n):
    return sorted(range(n), key=lambda i: -min(i, n - i))


LINE = [i for i in far_first(NZ) if i]
SLAB = [(dy, dc, dx) for dy in far_first(NY) for dx in far_first(NX) for dc in range(NC) if (dy, dc, dx) != (0, 0, 0)]
SLAB.sort(key=lambda o: -min(o[0], NY - o[0]) - min(o[2], NX - o[2]))
CORE = [o for o in SLAB if o[1] == 0]
FAR = [o for o in CORE if min(o[0], NY - o[0]) > 1]
NEAR = [o for o in CORE if o not in FAR]
FAR_SLOTS, NEAR_SLOTS = (2, 5), ((0, 2), (7, 1))
FAR_BLOCKS, NEAR_BLOCKS = 5 * NX, 3 * NX
BLOCK = 32
DELAY = [o for o in SLAB if o[2] == 0]
OTHER_X = [i for i in far_first(NX) if i]


def kernel(
    incident, onset, beta, inverse, matrix, history,
    currents, carried,
    onset_v, inc_v, hist_v, mat_v, inv_v, dl_v, stage_v, beta_v, first_v, res_v, base_v, zbuf, xbuf, c_own, c_all,
    passed, future,
    load_sem, send_sem, recv_sem, t_send, t_recv, z_send, z_recv, x_send, x_recv, c_send, c_recv, m_send, m_recv,
    p_send, p_recv, next_sem,
):
    d, r = lax.axis_index("delay"), lax.axis_index("row")
    y, c = d // NC, d % NC
    z, x = r // NX, r % NX

    def at(dy=0, dc=0, dz=0, dx=0):
        ty = lax.rem(y + dy, NY) if dy else y
        tc = 1 - c if dc else c
        tz = lax.rem(z + dz, NZ) if dz else z
        tx = lax.rem(x + dx, NX) if dx else x
        return (ty * NC + tc, tz * NX + tx)

    def remote(src, dst, send, recv, target):
        return pltpu.make_async_remote_copy(
            src_ref=src, dst_ref=dst, send_sem=send, recv_sem=recv, device_id=target, device_id_type=MESH
        )

    def arrived(ref, sem):
        pltpu.make_async_copy(ref, ref, sem).wait()

    left = arrived

    def rows_of(dx, dc):
        t = (lax.rem(x + dx, NX) if dx else x) * NC + (1 - c if dc else c)
        return pl.ds(pl.multiple_of(t * ROWS, ROWS), ROWS)

    own_rows = rows_of(0, 0)

    def stacked(wide):
        return jnp.concatenate([wide[:, :256], wide[:, 256:]], axis=0)

    def unstacked(tall):
        return jnp.concatenate([tall[:ROWS], tall[ROWS:]], axis=1)

    def halves(block):
        block = block.astype(F32).reshape(NX, NC, ROWS, 256)
        return block[:, 0].reshape(NX * ROWS, 256), block[:, 1].reshape(NX * ROWS, 256)

    def in_order(zeroth, first, width):
        parts = [v.reshape(NX, 1, ROWS, width) for v in (zeroth, first)]
        return jnp.concatenate(parts, axis=1).reshape(64, width)

    loads = [
        pltpu.make_async_copy(src, dst, load_sem.at[i])
        for i, (src, dst) in enumerate(
            ((onset, onset_v), (incident, inc_v), (history.at[0], hist_v), (beta, beta_v.at[c]), (matrix.at[0], mat_v))
        )
    ]
    for load in loads:
        load.start()

    barrier = pltpu.get_barrier_semaphore()
    for i in LINE:
        pl.semaphore_signal(barrier, inc=1, device_id=at(dz=i), device_id_type=MESH)
    for dy, dc, dx in SLAB:
        pl.semaphore_signal(barrier, inc=1, device_id=at(dy, dc, 0, dx), device_id_type=MESH)

    for load in loads[:4]:
        load.wait()

    @pl.when(d < STEPS)
    def _():
        row_of = lax.broadcasted_iota(jnp.int32, (8, 128), 0)
        start = []
        for i in range(0, 64, 8):
            group = jnp.zeros((8, 128), jnp.int32)
            for e in range(8):
                group = jnp.where(row_of == e, onset_v[i + e], group)
            start.append(group)
        offset = (d - jnp.concatenate(start, axis=0)).astype(F32)
        envelope = jnp.where(offset >= 0.0, jnp.exp(-((offset - 1.0) ** 2) / 4.0), 0.0)
        res_v[...] = inc_v[...].astype(F32) * envelope - hist_v[...]

    pl.semaphore_wait(barrier, len(LINE) + len(SLAB))


    def cut(k, half):
        for dy, dc, dx in DELAY:
            t, tr = at(dy, dc)
            rows = pl.ds(pl.multiple_of(t * 256 + half * 128, 128), 128)
            sems = send_sem.at[1], recv_sem.at[1 + 2 * k + half]
            remote(matrix.at[0, rows], stage_v.at[k, half], *sems, (t, tr)).start()
        rows = pl.ds(k * 256 + half * 128, 128)
        pltpu.make_async_copy(matrix.at[0, rows], stage_v.at[k, half], recv_sem.at[1 + 2 * k + half]).start()

    def forward(k, half):
        arrived(stage_v.at[k, half], recv_sem.at[1 + 2 * k + half])
        rows = pl.ds(pl.multiple_of(c * 256 + half * 128, 128), 128)
        landing = dl_v.at[k, rows, pl.ds(pl.multiple_of(x * 128, 128), 128)]
        for i in OTHER_X:
            remote(stage_v.at[k, half], landing, send_sem.at[4], recv_sem.at[7 + 2 * k + half], at(dx=i)).start()
        pltpu.make_async_copy(stage_v.at[k, half], landing, recv_sem.at[7 + 2 * k + half]).start()

    def to_mate(ref, i):
        remote(ref, ref, t_send.at[i], t_recv.at[i], at(dc=1)).start()

    def share_matrix(k):
        for half in range(2):
            rows = pl.ds(pl.multiple_of(c * 256 + half * 128, 128), 128)
            arrived(dl_v.at[k, rows], recv_sem.at[7 + 2 * k + half])
            to_mate(dl_v.at[k, rows], 2 + 2 * k + half)

    def have_matrix(k):
        for half in range(2):
            arrived(dl_v.at[k, pl.ds(0, 128)], t_recv.at[2 + 2 * k + half])

    to_mate(beta_v.at[c], 1)

    @pl.when(d == 0)
    def _():
        for dy, dc, dx in SLAB:
            t = at(dy, dc, 0, dx)
            remote(res_v.at[rows_of(dx, dc)], first_v.at[x], send_sem.at[0], recv_sem.at[0], t).start()
        pltpu.make_async_copy(res_v.at[own_rows], first_v.at[x], recv_sem.at[0]).start()
        cut(0, 0)
        cut(0, 1)

    inv_columns = pl.ds(pl.multiple_of(c * 256, 256), 256)
    inv_landing = inv_v.at[pl.ds(pl.multiple_of(x * 128, 128), 128), inv_columns]
    for i in OTHER_X:
        remote(inverse, inv_landing, send_sem.at[2], recv_sem.at[5], at(dx=i)).start()
    pltpu.make_async_copy(inverse, inv_landing, recv_sem.at[5]).start()

    @pl.when(jnp.logical_and(d > 0, d < STEPS))
    def _():
        for dy, dc, dx in SLAB:
            if dy == 0:
                remote(res_v.at[rows_of(dx, dc)], base_v.at[x], send_sem.at[3], recv_sem.at[6], at(0, dc, 0, dx)).start()
        pltpu.make_async_copy(res_v.at[own_rows], base_v.at[x], recv_sem.at[6]).start()

    def pass_on(src, k):
        @pl.when(d > 0)
        def _():
            remote(src, passed.at[k], p_send.at[k], p_recv.at[k], (jnp.maximum(d - 1, 0), r)).start()

    def take(k):
        @pl.when(d < ND - 1)
        def _():
            arrived(passed.at[k], p_recv.at[k])

        return jnp.where(d < ND - 1, passed[k], 0.0)

    slot_rows = pl.ds(pl.multiple_of(x * NC * ROWS, NC * ROWS), NC * ROWS)

    def send_values(s):
        for part, where in enumerate((FAR, NEAR)):
            for dy, dc, dx in where:
                landing = c_all.at[s, c, (NY - dy) % NY, slot_rows]
                remote(c_own.at[s], landing, c_send.at[s], c_recv.at[s, part], at(dy, 0, 0, dx)).start()
        pltpu.make_async_copy(c_own.at[s], c_all.at[s, c, 0, slot_rows], c_recv.at[s, 1]).start()

    def share(s, part):
        arrived(mat_v.at[pl.ds(0, FAR_BLOCKS * BLOCK if part == 0 else NEAR_BLOCKS * BLOCK)], c_recv.at[s, part])
        for slots in (FAR_SLOTS,) if part == 0 else NEAR_SLOTS:
            piece = c_all.at[s, c, pl.ds(*slots)]
            remote(piece, piece, m_send.at[s], m_recv.at[s, part], at(dc=1)).start()

    def multiply(s, part, core):
        total = jnp.zeros((NX * ROWS, 128), F32)
        for first, slots in (FAR_SLOTS,) if part == 0 else NEAR_SLOTS:
            for slot in range(first, first + slots):
                for half, values in enumerate(halves(c_all[s, core, slot])):
                    at_row = (NC * lax.rem(y + slot, NY) + half) * 256
                    rows = pl.ds(pl.multiple_of(at_row, 256), 256)
                    total += jnp.dot(values.astype(BF16), mat_v[rows], preferred_element_type=F32)
        return total

    def product(s):
        share(s, 0)
        own = multiply(s, 0, c)
        share(s, 1)
        own += multiply(s, 1, c)
        other = jnp.zeros((NX * ROWS, 128), F32)
        for part, blocks in enumerate((FAR_BLOCKS, NEAR_BLOCKS)):
            arrived(mat_v.at[pl.ds(0, blocks * BLOCK)], m_recv.at[s, part])
            other += multiply(s, part, 1 - c)
        columns = [jnp.where(c == 0, *halves(c_all[s, core, 0])) for core in range(NC)]
        currents[s] = in_order(*columns, 256).astype(BF16)
        return in_order(jnp.where(c == 0, own, other), jnp.where(c == 0, other, own), 128)

    def side_by_side(blocks):
        return jnp.concatenate([blocks[i].astype(F32) for i in range(NX)], axis=1)

    arrived(inv_v.at[:, inv_columns], recv_sem.at[5])
    to_mate(inv_v.at[:, inv_columns], 0)
    arrived(first_v, recv_sem.at[0])
    residual = side_by_side(first_v)
    for s in range(STEPS):
        if s == 0:
            arrived(inv_v.at[:, inv_columns], t_recv.at[0])
        partial_sum = jnp.dot(residual.astype(BF16), inv_v[...], preferred_element_type=F32)
        zbuf[s, z] = stacked(partial_sum).astype(BF16)
        for i in LINE:
            remote(zbuf.at[s, z], zbuf.at[s, z], z_send.at[s], z_recv.at[s], at(dz=i)).start()
        if s == 0:
            forward(0, 0)
            forward(0, 1)

            @pl.when(d == 0)
            def _():
                left(mat_v.at[pl.ds(0, (ND - 1) * 256)], send_sem.at[1])
                pl.semaphore_signal(next_sem, inc=1, device_id=at(dc=1), device_id_type=MESH)

            @pl.when(d == 1)
            def _():
                pl.semaphore_wait(next_sem, 1)
                cut(1, 0)
                cut(1, 1)


            @pl.when(y < STEPS - 1)
            def _():
                arrived(base_v, recv_sem.at[6])

            arrived(beta_v.at[c], t_recv.at[1])
            share_matrix(0)
            beta_wide = jnp.concatenate([jnp.broadcast_to(beta_v[i], (ROWS, 256)) for i in range(NC)], axis=0)

        if s == 1:
            pass_on(history.at[0], 0)
            send_values(0)
            share_matrix(1)
        if s == 2:
            send_values(1)
            loads[4].wait()
            future[0] = product(0) + take(0)
            pass_on(future.at[0], 1)

        arrived(zbuf.at[s, pl.ds(0, NZ - 1)], z_recv.at[s])
        solved = zbuf[s, 0].astype(F32)
        for i in range(1, NZ):
            solved += zbuf[s, i].astype(F32)
        current = (solved / (1.0 + beta_wide * solved * solved)).astype(BF16)
        c_own[s] = current
        if s < STEPS - 1:
            have_matrix(s)
            wide = unstacked(current.astype(F32)).astype(BF16)
            part = -jnp.dot(wide, dl_v[0], preferred_element_type=F32)
            if s == 0:
                earlier = wide
            else:
                part -= jnp.dot(earlier, dl_v[1], preferred_element_type=F32)
            part += jnp.where(y == s, side_by_side(base_v), 0.0)
            xbuf[s, y] = stacked(part).astype(BF16)
            for i in LINE:
                remote(xbuf.at[s, y], xbuf.at[s, y], x_send.at[s], x_recv.at[s], at(i)).start()

        if s == STEPS - 1:
            send_values(s)
        if s < STEPS - 1:
            if s == 0:
                forward(1, 0)
                forward(1, 1)
            arrived(xbuf.at[s, pl.ds(0, NY - 1)], x_recv.at[s])
            total = xbuf[s, 0].astype(F32)
            for i in range(1, NY):
                total += xbuf[s, i].astype(F32)
            residual = unstacked(total)

    future[1] = product(1)
    future[1] = future[1] + take(1)
    pass_on(future.at[1], 2)

    for s in range(STEPS):
        left(zbuf.at[s, pl.ds(0, NZ - 1)], z_send.at[s])
        if s < STEPS - 1:
            left(xbuf.at[s, pl.ds(0, NY - 1)], x_send.at[s])
            left(mat_v.at[pl.ds(0, len(CORE) * BLOCK)], c_send.at[s])
            left(c_all.at[s, c], m_send.at[s])

        @pl.when(d > 0)
        def _(s=s):
            left(passed.at[s], p_send.at[s])

    left(inv_v.at[pl.ds(0, (NX - 1) * 128), inv_columns], send_sem.at[2])
    left(inv_v.at[:, inv_columns], t_send.at[0])
    left(beta_v.at[c], t_send.at[1])
    for i in range(2, 6):
        left(dl_v.at[0, pl.ds(0, 128)], t_send.at[i])
    left(mat_v.at[pl.ds(0, 2 * (NX - 1) * 256)], send_sem.at[4])

    @pl.when(d == 0)
    def _():
        left(mat_v.at[pl.ds(0, len(SLAB) * 16)], send_sem.at[0])

    @pl.when(d == 1)
    def _():
        left(mat_v.at[pl.ds(0, (ND - 1) * 256)], send_sem.at[1])

    @pl.when(jnp.logical_and(d > 0, d < STEPS))
    def _():
        left(mat_v.at[pl.ds(0, (NX * NC - 1) * 16)], send_sem.at[3])

    total = product(2)
    carried[0] = total + take(2)
    left(mat_v.at[pl.ds(0, len(CORE) * BLOCK)], c_send.at[STEPS - 1])
    left(c_all.at[STEPS - 1, c], m_send.at[STEPS - 1])


def per_device(incident, onset, beta, inverse_block, delay_blocks, history_sum):
    hbm = pl.BlockSpec(memory_space=pltpu.HBM)
    vmem = pl.BlockSpec(memory_space=pltpu.VMEM)
    dma = pltpu.SemaphoreType.DMA
    steps = dma((STEPS,))
    return pl.pallas_call(
        kernel,
        out_shape=(
            pltpu.VMEM((STEPS, 64, 256), BF16),
            pltpu.VMEM((1, 64, 128), F32),
        ),
        in_specs=[hbm] * 6,
        out_specs=(vmem, vmem),
        scratch_shapes=[
            pltpu.SMEM((64,), jnp.int32),
            pltpu.VMEM((64, 128), BF16),
            pltpu.VMEM((64, 128), F32),
            pltpu.VMEM((4096, 128), BF16),
            pltpu.VMEM((512, 512), BF16),
            pltpu.VMEM((2, 512, 512), BF16),
            pltpu.VMEM((2, 2, 128, 128), BF16),
            pltpu.VMEM((NC, 1, 256), F32),
            pltpu.VMEM((NX, ROWS, 128), F32),
            pltpu.VMEM((64, 128), F32),
            pltpu.VMEM((NX, ROWS, 128), F32),
            pltpu.VMEM((STEPS, NZ, 16, 256), BF16),
            pltpu.VMEM((STEPS - 1, NY, 16, 256), BF16),
            pltpu.VMEM((STEPS, 16, 256), BF16),
            pltpu.VMEM((STEPS, NC, NY, 64, 256), BF16),
            pltpu.VMEM((STEPS, 64, 128), F32),
            pltpu.VMEM((STEPS - 1, 64, 128), F32),
            dma((5,)),
            dma((5,)),
            dma((11,)),
            dma((6,)),
            dma((6,)),
            *[steps] * 5,
            dma((STEPS, 2)),
            steps,
            dma((STEPS, 2)),
            *[steps] * 2,
            pltpu.SemaphoreType.REGULAR,
        ],
        compiler_params=pltpu.CompilerParams(
            collective_id=0, has_side_effects=True, vmem_limit_bytes=60 * 10**6
        ),
    )(incident, onset, beta.reshape(1, 256), inverse_block, delay_blocks, history_sum)


def solution(mesh):
    placed = (
        P(None, "row"),
        P(),
        P("delay"),
        P("row", "delay"),
        P("delay", None, "row"),
        P("delay", None, "row"),
    )
    return jax.shard_map(
        per_device,
        mesh=mesh,
        in_specs=placed,
        out_specs=(P(None, None, "delay"), P("delay", None, "row")),
        check_vma=False,
    )
```
